256 devices in a mesh: dp: 16 (over y_lo, x, core), tensor: 16 (over y_hi, z).
Axes of the slice: x: 4, y: 4 (y_hi: 2, y_lo: 2; y = y_hi * 2 + y_lo), z: 8, core: 2. Of those that a mesh axis runs over, the one named last changes fastest.
Arguments:
- sublayer_input: bfloat16 [4096, 6144], P('dp'), may hold values from -6 to 6
- w_qkv: bfloat16 [6144, 32, 384], P('dp', 'tensor'), may hold values from -0.078125 to 0.078125
- w_out: bfloat16 [6144, 32, 128], P('dp', 'tensor'), may hold values from -0.5 to 0.5
- upstream_grad: bfloat16 [4096, 6144], P('dp'), may hold values from -6 to 6
Outputs:
- hidden_input_gradient: bfloat16 [4096, 6144], P(('dp', 'tensor'))
- grad_qkv: float32 [6144, 32, 384], P('dp', 'tensor')
- grad_out: float32 [6144, 32, 128], P('dp', 'tensor')
The draws below stay inside these ranges and needn't reach their ends.
All inputs are finite; a program needn't handle non-finite values.
Results may differ from the reference program's by a relative error of at most 0.023.
Values may be sent and summed in bfloat16 or wider, within the bound.
A program may use at most 128 MiB of HBM per device.

```python
import math
import jax
import jax.numpy as jnp
from jax import lax

D = 6144
HEAD = 128
SEQ = 256
HEADS = 32
TOKENS = 4096
N_DP = 16
N_TENSOR = 16


def spiked(drawn, key, source, target, parts, factor):
    owner, partner = [(jnp.arange(drawn.shape[dim]) // (drawn.shape[dim] // parts)).reshape([-1 if axis == dim else 1 for axis in range(drawn.ndim)]) for dim in (source, target)]
    chosen = jax.random.permutation(key, parts)[partner]
    strong = (owner == chosen) | (owner == (partner + parts // 2) % parts)
    return jnp.where(strong, factor * drawn, drawn)


def level_of(own_key, dims, shards, low, top_value):
    factor_of, own = 1.0, jax.random.fold_in(own_key, 6)
    for axis_at, shards_of in shards:
        heights = jnp.exp(jax.random.uniform(jax.random.fold_in(own, axis_at), (shards_of,), jnp.float32, low / len(shards), top_value / len(shards)))
        factor_of = factor_of * jnp.repeat(heights, dims[axis_at] // shards_of).reshape([-1 if axis == axis_at else 1 for axis in range(len(dims))])
    return factor_of


def bell_draw(stream_key, dims, deviation, reach, split=(), held_as=jnp.bfloat16):
    gain = level_of(stream_key, dims, split, -0.22, 0.18) if split else 1.0
    entries = jax.random.normal(stream_key, dims, jnp.float32) * deviation * gain
    return jnp.minimum(jnp.maximum(entries, -reach), reach).astype(held_as)


def heavy_noise(stream_key, shape, deviation, most, cuts, heavy, held_as=jnp.bfloat16):
    array = deviation * jax.random.normal(stream_key, shape, jnp.float32)
    if cuts:
        array = array * level_of(stream_key, shape, cuts, -0.22, 0.18)
    return jnp.clip(spiked(array, jax.random.fold_in(stream_key, 3), *heavy), -most, most).astype(held_as)


def setup_inputs(seed: int = 0) -> dict:
    arg_keys = jax.random.split(jax.random.key(seed), 5)
    sublayer_input = bell_draw(arg_keys[0], (TOKENS, D), 1.0, 6.0, ((0, 16),))
    w_qkv = bell_draw(arg_keys[1], (D, HEADS, 3 * HEAD), D ** -0.5, 0.078125, ((0, 16), (1, 16)))
    w_out = bell_draw(arg_keys[2], (D, HEADS, HEAD), HEAD ** -0.5, 0.5, ((0, 16), (1, 16)))
    upstream_grad = heavy_noise(arg_keys[3], (TOKENS, D), 1.0, 6.0, ((0, 16),), (0, 1, 16, 2.0))
    return {"sublayer_input": sublayer_input, "w_qkv": w_qkv, "w_out": w_out, "upstream_grad": upstream_grad}


EPS = 1e-05

def rounded(values):
    return lax.optimization_barrier(values.astype(jnp.bfloat16)).astype(jnp.float32)

def apply_layer_norm(hidden_rows):
    hidden_rows = hidden_rows.astype(jnp.float32)
    centered = hidden_rows - lax.optimization_barrier(jnp.mean(hidden_rows, axis=-1, keepdims=True))
    inverse_deviation = lax.rsqrt(lax.optimization_barrier(jnp.mean(centered * centered, axis=-1, keepdims=True)) + EPS)
    return (centered * inverse_deviation, inverse_deviation)

def reference(sublayer_input, w_qkv, w_out, upstream_grad):
    token_count, model_width = sublayer_input.shape
    head_count = w_qkv.shape[1]
    head_width = w_out.shape[2]
    seq_count = token_count // SEQ
    score_scale = 1.0 / math.sqrt(head_width)
    standardized_input, inverse_deviation = apply_layer_norm(sublayer_input)
    normalized_rows = standardized_input.astype(jnp.bfloat16)
    flat_qkv = w_qkv.reshape(model_width, head_count * 3 * head_width)
    flat_out = w_out.reshape(model_width, head_count * head_width)
    qkv = rounded(jnp.dot(normalized_rows, flat_qkv, preferred_element_type=jnp.float32))
    qkv = qkv.reshape(seq_count, SEQ, head_count, 3 * head_width)
    queries = qkv[..., :head_width]
    key_part = qkv[..., head_width:2 * head_width]
    value_part = qkv[..., 2 * head_width:]
    scores = jnp.einsum('bqhe,bkhe->bhqk', queries, key_part) * score_scale
    raised = jnp.exp(scores)
    attn_probs = raised / lax.optimization_barrier(jnp.sum(raised, axis=-1, keepdims=True))
    probs_b = rounded(attn_probs)
    context = rounded(jnp.einsum('bhqk,bkhe->bqhe', probs_b, value_part))
    grad_context = rounded(jnp.dot(upstream_grad, flat_out, preferred_element_type=jnp.float32))
    context_flat = context.reshape(token_count, head_count * head_width).astype(jnp.bfloat16)
    grad_out = jnp.dot(upstream_grad.T, context_flat, preferred_element_type=jnp.float32) / N_DP
    grad_out = grad_out.reshape(model_width, head_count, head_width)
    grad_context = grad_context.reshape(seq_count, SEQ, head_count, head_width)
    grad_prob = jnp.einsum('bqhe,bkhe->bhqk', grad_context, value_part)
    row_dot = lax.optimization_barrier(jnp.sum(attn_probs * grad_prob, axis=-1, keepdims=True))
    grad_score = rounded(attn_probs * (grad_prob - row_dot) * score_scale)
    grad_values = rounded(jnp.einsum('bhqk,bqhe->bkhe', probs_b, grad_context))
    grad_queries = rounded(jnp.einsum('bhqk,bkhe->bqhe', grad_score, key_part))
    grad_keys = rounded(jnp.einsum('bhqk,bqhe->bkhe', grad_score, queries))
    grad_rows = jnp.concatenate([grad_queries, grad_keys, grad_values], axis=-1)
    grad_rows = grad_rows.reshape(token_count, head_count * 3 * head_width).astype(jnp.bfloat16)
    grad_qkv = jnp.dot(normalized_rows.T, grad_rows, preferred_element_type=jnp.float32) / N_DP
    grad_qkv = grad_qkv.reshape(model_width, head_count, 3 * head_width)
    group_span = head_count // N_TENSOR * 3 * head_width

    def add_group(running, group_index):
        offset = (group_index * group_span).astype(jnp.int32)
        part_rows = lax.dynamic_slice_in_dim(grad_rows, offset, group_span, 1)
        part_weights = lax.dynamic_slice_in_dim(flat_qkv, offset, group_span, 1)
        term = jnp.dot(part_rows, part_weights.T, preferred_element_type=jnp.float32)
        return (running + rounded(term), None)
    normalized_rows_gradient, _ = lax.scan(add_group, jnp.zeros((token_count, model_width), jnp.float32), jnp.arange(N_TENSOR, dtype=jnp.int32))
    gradient_average = lax.optimization_barrier(jnp.mean(normalized_rows_gradient, axis=-1, keepdims=True))
    projection_average = lax.optimization_barrier(jnp.mean(normalized_rows_gradient * standardized_input, axis=-1, keepdims=True))
    hidden_input_gradient = (inverse_deviation * (normalized_rows_gradient - gradient_average - standardized_input * projection_average)).astype(jnp.bfloat16)
    return (hidden_input_gradient, grad_qkv, grad_out)
```

```python
import math

import jax
import jax.numpy as jnp
from jax import lax
from jax.experimental import pallas as pl
from jax.experimental.pallas import tpu as pltpu
from jax.sharding import PartitionSpec as P

EPS = 1e-05
MESH = pl.DeviceIdType.MESH
BF16 = jnp.bfloat16
F32 = jnp.float32

D = 6144
ROWS = 384
SEQ = 256
HEAD = 128
CHIP_D = 2 * ROWS
QW = 3 * HEAD
N_CHIPS = 8
N_DP = 16
GROUPS = 4
N_MESSAGES = 200

GATHER_A, GATHER_A0, GATHER_B0 = 160, 80, 112
SCATTER_A = {QW: 160, HEAD: 48}


def mm(a, b):
    return lax.dot_general(a, b, (((1,), (0,)), ((), ())), preferred_element_type=F32)


def mm_nt(a, b):
    return lax.dot_general(a, b, (((1,), (1,)), ((), ())), preferred_element_type=F32)


def standardize(rows):
    centered = rows - jnp.mean(rows, axis=-1, keepdims=True)
    inverse_deviation = lax.rsqrt(jnp.mean(centered * centered, axis=-1, keepdims=True) + EPS)
    return centered * inverse_deviation, inverse_deviation


def kernel(
    x_hbm, wq_hbm, wo_hbm, up_hbm,
    hid_out, gq_out, go_out,
    wq, wo, nrm, up, xbuf, xrow, acc_q, acc_o, qkv, probs, rows_t, rows, ctx_t,
    gq, go,
    q_ya, q_xa1, q_xa2, q_xb1, q_xb2, q_yb,
    o_ya, o_xa1, o_xa2, o_xb1, o_xb2, o_yb,
    sq_send, sq_recv, so_send, so_recv,
    gn, gns, gnr, zr0, zr1, ysend, yrecv, gnf, xhat, inv,
    local_sem, send_sem, recv_sem,
):
    dp = lax.axis_index("dp")
    tn = lax.axis_index("tensor")
    core = lax.rem(dp, 2)
    other = 1 - core
    x = lax.rem(lax.div(dp, 2), 4)
    y = lax.div(dp, 8)
    z = lax.rem(tn, 8)
    yh = lax.div(tn, 8)

    def dp_at(yy, xx, cc):
        return (yy * 4 + xx) * 2 + cc

    sib = (dp_at(y, x, other), tn)
    xp = (dp_at(y, lax.rem(x + 1, 4), core), tn)
    xm = (dp_at(y, lax.rem(x + 3, 4), core), tn)
    yp = (dp_at(1 - y, x, core), tn)
    zp = (dp, yh * 8 + lax.rem(z + 1, 8))
    zm = (dp, yh * 8 + lax.rem(z + 7, 8))
    yhp = (dp, (1 - yh) * 8 + z)
    partners = (sib, xp, xm, yp, zp, zm, yhp)

    messages = []

    def send(src, dst, target):
        k = len(messages)
        copy = pltpu.make_async_remote_copy(
            src_ref=src, dst_ref=dst, send_sem=send_sem.at[k], recv_sem=recv_sem.at[k],
            device_id=target, device_id_type=MESH,
        )
        copy.start()
        messages.append(copy)
        return copy

    def chip_cols(slot):
        dy, dx = lax.div(slot, 4), lax.rem(slot, 4)
        chip = lax.rem(y + dy, 2) * 4 + lax.rem(x + dx, 4)
        return pl.ds(pl.multiple_of(chip * CHIP_D, 128), CHIP_D)

    def add_rows(n_rows, dst, *srcs):
        def body(r, carry):
            at = pl.ds(pl.multiple_of(r * 16, 16), 16)
            total = dst(at)[...].astype(F32)
            for src in srcs:
                total = total + src(at)[...].astype(F32)
            dst(at)[...] = total.astype(BF16)
            return carry

        lax.fori_loop(0, n_rows // 16, body, 0)

    barrier = pltpu.get_barrier_semaphore()
    for partner in partners:
        pl.semaphore_signal(barrier, inc=1, device_id=partner, device_id_type=MESH)
    token0 = pl.multiple_of(tn * 16, 16)
    loads = [
        pltpu.make_async_copy(x_hbm, xbuf, local_sem.at[0]),
        pltpu.make_async_copy(x_hbm.at[pl.ds(token0, 16)], xrow, local_sem.at[1]),
        pltpu.make_async_copy(wq_hbm.at[core], wq.at[0, core], local_sem.at[2]),
        pltpu.make_async_copy(wo_hbm.at[core], wo.at[0, core], local_sem.at[3]),
        pltpu.make_async_copy(up_hbm, up.at[0], local_sem.at[4]),
    ]
    for load in loads[:4]:
        load.start()
    pl.semaphore_wait(barrier, len(partners))

    A = pl.ds(0, GATHER_A)
    A0 = pl.ds(0, GATHER_A0)
    A1 = pl.ds(GATHER_A0, GATHER_A - GATHER_A0)
    B = pl.ds(GATHER_A, ROWS - GATHER_A)
    B0 = pl.ds(GATHER_A, GATHER_B0)
    B1 = pl.ds(GATHER_A + GATHER_B0, ROWS - GATHER_A - GATHER_B0)

    class Gather:
        def __init__(self, w, w_hbm, load):
            self.w, self.w_hbm, self.load = w, w_hbm, load

        def stage0(self):
            w, src = self.w, self.w_hbm
            self.swap = send(src.at[other], w.at[0, core], sib)
            self.xa_p = [send(src.at[core, A], w.at[3, core, A], xp)]
            self.xa_m = [send(src.at[core, A], w.at[1, core, A], xm)]
            self.yb = [send(src.at[core, B], w.at[4, core, B], yp)]

        def stage0b(self):
            w = self.w
            self.swap.wait_recv()
            self.xa_p.append(send(w.at[0, other, A], w.at[3, other, A], xp))
            self.xa_m.append(send(w.at[0, other, A], w.at[1, other, A], xm))
            self.yb.append(send(w.at[0, other, B], w.at[4, other, B], yp))
            self.load.wait()
            self.xb_p = send(w.at[0, :, B], w.at[3, :, B], xp)
            self.xb_m = send(w.at[0, :, B], w.at[1, :, B], xm)
            self.ya = [send(w.at[0, :, A], w.at[4, :, A], yp)]

        def stage1(self):
            w = self.w
            for m in self.xa_p:
                m.wait_recv()
            self.xa2_p = send(w.at[3, :, A0], w.at[2, :, A0], xp)
            for m in self.xa_m:
                m.wait_recv()
            self.xa2_m = send(w.at[1, :, A1], w.at[2, :, A1], xm)
            self.ya.append(send(w.at[3, :, A], w.at[7, :, A], yp))
            self.ya.append(send(w.at[1, :, A], w.at[5, :, A], yp))

        def stage2(self):
            w = self.w
            for m in self.yb:
                m.wait_recv()
            self.xb3_p = send(w.at[4, :, B], w.at[7, :, B], xp)
            self.xb3_m = send(w.at[4, :, B], w.at[5, :, B], xm)

        def stage3(self):
            w = self.w
            self.xb_p.wait_recv()
            self.xb2_p = send(w.at[3, :, B0], w.at[2, :, B0], xp)
            self.xb_m.wait_recv()
            self.xb2_m = send(w.at[1, :, B1], w.at[2, :, B1], xm)

        def stage4(self):
            w = self.w
            self.xa2_p.wait_recv()
            self.ya.append(send(w.at[2, :, A0], w.at[6, :, A0], yp))
            self.xa2_m.wait_recv()
            self.ya.append(send(w.at[2, :, A1], w.at[6, :, A1], yp))

        def stage5(self):
            w = self.w
            self.xb3_p.wait_recv()
            self.xb4_p = send(w.at[7, :, B0], w.at[6, :, B0], xp)
            self.xb3_m.wait_recv()
            self.xb4_m = send(w.at[5, :, B1], w.at[6, :, B1], xm)

        def finish(self):
            for m in (self.xb2_p, self.xb2_m, *self.ya, self.xb4_p, self.xb4_m):
                m.wait_recv()

    g_q = Gather(wq, wq_hbm, loads[2])
    g_o = Gather(wo, wo_hbm, loads[3])
    g_q.stage0()
    g_q.stage0b()

    loads[4].start()
    up_msg = send(up_hbm, up.at[1], sib)
    loads[0].wait()

    def norm_rows(r, carry):
        at = pl.ds(pl.multiple_of(r * 16, 16), 16)
        standardized, _ = standardize(xbuf[at, :].astype(F32))
        nrm[0, at, :] = standardized.astype(BF16)
        return carry

    lax.fori_loop(0, SEQ // 16, norm_rows, 0)
    nrm_msg = send(nrm.at[0], nrm.at[1], sib)

    g_q.stage1()
    g_q.stage2()

    loads[1].wait()
    own_xhat, own_inv = standardize(xrow[...].astype(F32))
    xhat[...] = own_xhat
    inv[...] = jnp.broadcast_to(own_inv, (16, 128))

    g_q.stage3()
    g_o.stage0()
    g_o.stage0b()
    g_q.stage4()
    g_q.stage5()
    nrm_msg.wait_recv()
    g_q.finish()

    def project(acc, w, left, width):
        acc[...] = jnp.zeros_like(acc)

        def body(slot, carry):
            a = left[:, :, chip_cols(slot)].reshape(2 * SEQ, CHIP_D)
            b = w[slot].reshape(CHIP_D, width)
            acc[...] += mm(a, b)
            return carry

        lax.fori_loop(0, N_CHIPS, body, 0)

    project(acc_q, wq, nrm, QW)
    qkv[...] = acc_q[...].astype(BF16)
    g_o.stage1()
    g_o.stage2()

    scale = 1.0 / math.sqrt(HEAD)

    def forward(s):
        at = pl.ds(s * SEQ, SEQ)
        query, key, value = (qkv[at, pl.ds(n * HEAD, HEAD)] for n in range(3))
        raised = jnp.exp(mm_nt(query, key) * scale)
        attn = raised / jnp.sum(raised, axis=-1, keepdims=True)
        probs[s] = attn
        context = mm(attn.astype(BF16), value).astype(BF16).astype(F32)
        ctx_t[:, at] = context.T.astype(BF16)

    forward(0)
    g_o.stage3()
    g_o.stage4()
    forward(1)
    g_o.stage5()

    loads[4].wait()
    up_msg.wait_recv()

    def weight_unit(g, left_t, right, slot):
        b = right[:, :, chip_cols(slot)].reshape(2 * SEQ, CHIP_D)
        g[slot] = mm(left_t[...], b).astype(BF16)

    L = (pl.ds(0, ROWS), pl.ds(ROWS, ROWS))

    class Scatter:
        def __init__(self, g, width, ya, xa1, xa2, xb1, xb2, yb):
            self.g, self.width = g, width
            self.na = SCATTER_A[width]
            self.nb = width - self.na
            self.A, self.B = pl.ds(0, self.na), pl.ds(self.na, self.nb)
            self.ya, self.xa1, self.xa2, self.xb1, self.xb2, self.yb = ya, xa1, xa2, xb1, xb2, yb
            self.m = {}

        def rows_a(self, slot, lanes=slice(None)):
            return lambda at: self.g.at[slot, at, lanes]

        def rows_b(self, slot, lanes=slice(None)):
            def view(at):
                return self.g.at[slot, pl.ds(pl.multiple_of(at.start + self.na, 16), 16), lanes]

            return view

        def send_ya(self, dx):
            self.m["ya", dx] = send(self.g.at[4 + dx, self.A], self.ya.at[dx], yp)

        def send_xb1(self, dy):
            for n, target in enumerate((xp, xm)):
                self.m["xb1", dy, n] = send(
                    self.g.at[dy * 4 + 2, self.B, L[n]], self.xb1.at[dy, n], target
                )

        def step_xb2(self, dy):
            for n, (slot, target) in enumerate(((1, xp), (3, xm))):
                self.m["xb1", dy, n].wait_recv()
                add_rows(
                    self.nb, self.rows_b(dy * 4 + slot, L[n]),
                    lambda at, n=n: self.xb1.at[dy, n, at],
                )
                self.m["xb2", dy, n] = send(
                    self.g.at[dy * 4 + slot, self.B], self.xb2.at[dy, n], target
                )

        def step_xa1(self):
            self.m["ya", 2].wait_recv()
            add_rows(self.na, self.rows_a(2), lambda at: self.ya.at[2, at])
            for n, target in enumerate((xp, xm)):
                self.m["xa1", n] = send(self.g.at[2, self.A, L[n]], self.xa1.at[n], target)

        def step_xa2(self):
            for n, (slot, target) in enumerate(((1, xp), (3, xm))):
                self.m["ya", slot].wait_recv()
                self.m["xa1", n].wait_recv()
                add_rows(
                    self.na, self.rows_a(slot, L[n]),
                    lambda at, n=n, slot=slot: self.ya.at[slot, at, L[n]],
                    lambda at, n=n: self.xa1.at[n, at],
                )
                add_rows(
                    self.na, self.rows_a(slot, L[1 - n]),
                    lambda at, n=n, slot=slot: self.ya.at[slot, at, L[1 - n]],
                )
                self.m["xa2", n] = send(self.g.at[slot, self.A], self.xa2.at[n], target)

        def step_yb(self):
            for n in range(2):
                self.m["xb2", 1, n].wait_recv()
            add_rows(
                self.nb, self.rows_b(4),
                lambda at: self.xb2.at[1, 0, at], lambda at: self.xb2.at[1, 1, at],
            )
            self.m["yb"] = send(self.g.at[4, self.B], self.yb, yp)

        def finish(self, out, out_stride, send_buf, recv_buf):
            for key in (("xb2", 0, 0), ("xb2", 0, 1), ("ya", 0), ("xa2", 0), ("xa2", 1), "yb"):
                self.m[key].wait_recv()

            def total(lanes):
                a = self.g[0, self.A, lanes].astype(F32) + self.ya[0, :, lanes].astype(F32)
                a = a + self.xa2[0, :, lanes].astype(F32) + self.xa2[1, :, lanes].astype(F32)
                b = self.g[0, self.B, lanes].astype(F32) + self.yb[:, lanes].astype(F32)
                b = b + self.xb2[0, 0, :, lanes].astype(F32) + self.xb2[0, 1, :, lanes].astype(F32)
                return jnp.concatenate([a, b], axis=0) * (1.0 / N_DP)

            def lanes_of(cc):
                return pl.ds(pl.multiple_of(cc * ROWS, 128), ROWS)

            send_buf[...] = total(lanes_of(other)).astype(BF16)
            message = send(send_buf, recv_buf, sib)

            def write(value, head):
                for fb in range(self.width // HEAD):
                    block = value[fb * HEAD:(fb + 1) * HEAD, :].T
                    out[pl.ds(fb * 2 + head, ROWS, stride=out_stride), :] = block

            write(total(lanes_of(core)), core)
            message.wait_recv()
            write(recv_buf[...].astype(F32), other)

    s_o = Scatter(go, HEAD, o_ya, o_xa1, o_xa2, o_xb1, o_xb2, o_yb)
    s_q = Scatter(gq, QW, q_ya, q_xa1, q_xa2, q_xb1, q_xb2, q_yb)

    def go_body(slot, carry):
        weight_unit(go, ctx_t, up, slot)
        return carry

    lax.fori_loop(0, N_CHIPS, go_body, 0)
    for dy in range(2):
        s_o.send_xb1(dy)
    for dx in (2, 1, 3, 0):
        s_o.send_ya(dx)

    g_o.finish()
    project(acc_o, wo, up, HEAD)

    def backward(s):
        at = pl.ds(s * SEQ, SEQ)
        query, key, value = (qkv[at, pl.ds(n * HEAD, HEAD)] for n in range(3))
        grad_context = acc_o[at, :].astype(BF16)
        attn = probs[s]
        grad_prob = mm_nt(grad_context, value)
        row_dot = jnp.sum(attn * grad_prob, axis=-1, keepdims=True)
        grad_score = (attn * (grad_prob - row_dot) * scale).astype(BF16)
        query_t = query.astype(F32).T.astype(BF16)
        key_t = key.astype(F32).T.astype(BF16)
        grad_context_t = grad_context.astype(F32).T.astype(BF16)
        parts = (
            mm_nt(key_t, grad_score),
            mm(query_t, grad_score),
            mm(grad_context_t, attn.astype(BF16)),
        )
        for n, part in enumerate(parts):
            rows_t[pl.ds(n * HEAD, HEAD), at] = part.astype(BF16)
            rows[at, pl.ds(n * HEAD, HEAD)] = part.T.astype(BF16)

    backward(0)
    s_o.step_xb2(0)
    backward(1)

    def gn_group(g):
        for slot in (2 * g, 2 * g + 1):
            part = mm_nt(rows[...], wq[slot].reshape(CHIP_D, QW)).astype(BF16)
            gn[slot] = part[:SEQ].reshape(2, 128, CHIP_D)
            gns[slot] = part[SEQ:].reshape(2, 128, CHIP_D)
        return send(gns.at[pl.ds(2 * g, 2)], gnr.at[pl.ds(2 * g, 2)], sib)

    def z_rows(dz):
        return pl.ds(pl.multiple_of(lax.rem(z + dz + 8, 8) * 16, 16), 16)

    zm_msgs = {}
    directions = ((zp, 1), (zm, -1))

    def gn_step0(g, message):
        message.wait_recv()
        for slot in (2 * g, 2 * g + 1):
            for h in range(2):
                add_rows(
                    128, lambda at, slot=slot, h=h: gn.at[slot, h, at],
                    lambda at, slot=slot, h=h: gnr.at[slot, h, at],
                )
        for n, (target, _) in enumerate(directions):
            zm_msgs[g, 0, n] = send(gn.at[2 * g + n, :, z_rows(4)], zr0.at[n, g], target)

    def gn_step(g, step):
        for n, (target, sign) in enumerate(directions):
            at = z_rows(sign * (4 - step))
            zm_msgs[g, step - 1, n].wait_recv()
            if step == 1:
                mine = gn[2 * g + n, :, at, :].astype(F32)
                gn[2 * g + n, :, at, :] = (mine + zr0[n, g].astype(F32)).astype(BF16)
            else:
                mine = gn[pl.ds(2 * g, 2), :, at, :].astype(F32)
                mine = mine + zr1[n, g, step - 2].astype(F32)
                gn[pl.ds(2 * g, 2), :, at, :] = mine.astype(BF16)
            zm_msgs[g, step, n] = send(
                gn.at[pl.ds(2 * g, 2), :, at], zr1.at[n, g, step - 1], target
            )

    def gn_sum(g, which):
        at = z_rows(0)
        pair = pl.ds(2 * g, 2)
        total = gn[pair, which, at, :].astype(F32)
        return total + zr1[0, g, 2, :, which].astype(F32) + zr1[1, g, 2, :, which].astype(F32)

    def gn_exchange(g):
        for n in range(2):
            zm_msgs[g, 3, n].wait_recv()
        ysend[g] = gn_sum(g, 1 - yh).astype(BF16)
        zm_msgs[g, "y"] = send(ysend.at[g], yrecv.at[g], yhp)

    def gn_finish(g):
        zm_msgs[g, "y"].wait_recv()
        total = gn_sum(g, yh) + yrecv[g].astype(F32)
        for n in range(2):
            gnf[:, chip_cols(jnp.int32(2 * g + n))] = total[n]

    def q_units(*slots):
        for slot in slots:
            weight_unit(gq, rows_t, nrm, jnp.int32(slot))

    m0 = gn_group(0)
    q_units(2, 6)
    s_q.send_xb1(0)
    s_q.send_xb1(1)
    s_q.send_ya(2)
    gn_step0(0, m0)
    m1 = gn_group(1)
    s_o.step_xb2(1)
    q_units(5, 7)
    s_q.send_ya(1)
    s_q.send_ya(3)
    gn_step0(1, m1)
    m2 = gn_group(2)
    s_o.step_xa1()
    q_units(1, 3)
    gn_step0(2, m2)
    m3 = gn_group(3)
    s_o.step_xa2()
    q_units(4, 0)
    s_q.send_ya(0)
    gn_step0(3, m3)
    s_o.step_yb()

    gn_step(0, 1)
    gn_step(1, 1)
    s_q.step_xb2(0)
    s_q.step_xb2(1)
    gn_step(2, 1)
    gn_step(3, 1)
    s_q.step_xa1()
    gn_step(0, 2)
    gn_step(1, 2)
    s_q.step_xa2()
    gn_step(2, 2)
    gn_step(3, 2)
    s_o.finish(go_out, 2, so_send, so_recv)
    gn_step(0, 3)
    gn_step(1, 3)
    s_q.step_yb()
    gn_step(2, 3)
    gn_step(3, 3)
    gn_exchange(0)
    gn_exchange(1)
    s_q.finish(gq_out, 6, sq_send, sq_recv)
    gn_exchange(2)
    gn_exchange(3)
    for g in range(GROUPS):
        gn_finish(g)

    total = gnf[...]
    standardized = xhat[...]
    mean_g = jnp.mean(total, axis=-1, keepdims=True)
    mean_p = jnp.mean(total * standardized, axis=-1, keepdims=True)
    hid_out[...] = (inv[:, :1] * (total - mean_g - standardized * mean_p)).astype(BF16)

    for message in messages:
        message.wait_send()


def scatter_buffers(width):
    a = SCATTER_A[width]
    b = width - a
    return [
        pltpu.VMEM((4, a, CHIP_D), BF16),
        pltpu.VMEM((2, a, ROWS), BF16),
        pltpu.VMEM((2, a, CHIP_D), BF16),
        pltpu.VMEM((2, 2, b, ROWS), BF16),
        pltpu.VMEM((2, 2, b, CHIP_D), BF16),
        pltpu.VMEM((b, CHIP_D), BF16),
    ]


def per_device(sublayer_input, w_qkv, w_out, upstream_grad):
    wq = jnp.transpose(w_qkv, (1, 0, 2))
    wo = jnp.transpose(w_out, (1, 0, 2))
    scratch = [
        pltpu.VMEM((N_CHIPS, 2, ROWS, QW), BF16),
        pltpu.VMEM((N_CHIPS, 2, ROWS, HEAD), BF16),
        pltpu.VMEM((2, SEQ, D), BF16),
        pltpu.VMEM((2, SEQ, D), BF16),
        pltpu.VMEM((SEQ, D), BF16),
        pltpu.VMEM((16, D), BF16),
        pltpu.VMEM((2 * SEQ, QW), F32),
        pltpu.VMEM((2 * SEQ, HEAD), F32),
        pltpu.VMEM((2 * SEQ, QW), BF16),
        pltpu.VMEM((2, SEQ, SEQ), F32),
        pltpu.VMEM((QW, 2 * SEQ), BF16),
        pltpu.VMEM((2 * SEQ, QW), BF16),
        pltpu.VMEM((HEAD, 2 * SEQ), BF16),
        pltpu.VMEM((N_CHIPS, QW, CHIP_D), BF16),
        pltpu.VMEM((N_CHIPS, HEAD, CHIP_D), BF16),
        *scatter_buffers(QW),
        *scatter_buffers(HEAD),
        pltpu.VMEM((QW, ROWS), BF16),
        pltpu.VMEM((QW, ROWS), BF16),
        pltpu.VMEM((HEAD, ROWS), BF16),
        pltpu.VMEM((HEAD, ROWS), BF16),
        pltpu.VMEM((N_CHIPS, 2, 128, CHIP_D), BF16),
        pltpu.VMEM((N_CHIPS, 2, 128, CHIP_D), BF16),
        pltpu.VMEM((N_CHIPS, 2, 128, CHIP_D), BF16),
        pltpu.VMEM((2, GROUPS, 2, 16, CHIP_D), BF16),
        pltpu.VMEM((2, GROUPS, 3, 2, 2, 16, CHIP_D), BF16),
        pltpu.VMEM((GROUPS, 2, 16, CHIP_D), BF16),
        pltpu.VMEM((GROUPS, 2, 16, CHIP_D), BF16),
        pltpu.VMEM((16, D), F32),
        pltpu.VMEM((16, D), F32),
        pltpu.VMEM((16, 128), F32),
        pltpu.SemaphoreType.DMA((5,)),
        pltpu.SemaphoreType.DMA((N_MESSAGES,)),
        pltpu.SemaphoreType.DMA((N_MESSAGES,)),
    ]
    any_spec = pl.BlockSpec(memory_space=pl.ANY)
    vmem_spec = pl.BlockSpec(memory_space=pltpu.VMEM)
    hid, gq, go = pl.pallas_call(
        kernel,
        out_shape=(
            jax.ShapeDtypeStruct((16, D), BF16),
            jax.ShapeDtypeStruct((ROWS * 6, HEAD), F32),
            jax.ShapeDtypeStruct((ROWS * 2, HEAD), F32),
        ),
        in_specs=[any_spec] * 4,
        out_specs=(vmem_spec,) * 3,
        scratch_shapes=scratch,
        compiler_params=pltpu.CompilerParams(
            collective_id=0, has_side_effects=True, vmem_limit_bytes=62 * 2**20
        ),
        cost_estimate=pl.CostEstimate(
            flops=10_000_000_000, bytes_accessed=10_000_000, transcendentals=200_000
        ),
    )(sublayer_input, wq, wo, upstream_grad)
    gq = gq.reshape(ROWS, 3, 2, HEAD).transpose(0, 2, 1, 3).reshape(ROWS, 2, QW)
    go = go.reshape(ROWS, 2, HEAD)
    return hid, gq, go


def solution(mesh):
    in_specs = (P("dp", None), P("dp", "tensor", None), P("dp", "tensor", None), P("dp", None))
    out_specs = (P(("dp", "tensor"), None), P("dp", "tensor", None), P("dp", "tensor", None))
    return jax.shard_map(
        per_device, mesh=mesh, in_specs=in_specs, out_specs=out_specs, check_vma=False
    )
```

```python
import math

import jax
import jax.numpy as jnp
from jax import lax
from jax.experimental import pallas as pl
from jax.experimental.pallas import tpu as pltpu
from jax.sharding import PartitionSpec as P

EPS = 1e-05
MESH = pl.DeviceIdType.MESH
BF16 = jnp.bfloat16
F32 = jnp.float32

D = 6144
ROWS = 384
SEQ = 256
HEAD = 128
CHIP_D = 2 * ROWS
QW = 3 * HEAD
N_CHIPS = 8
N_DP = 16
GROUPS = 4
N_MESSAGES = 200
SLOT_ORDER = (0, 3, 1, 4, 7, 5, 2, 6)

GATHER_A, GATHER_A0, GATHER_B0 = 160, 80, 112
SCATTER_A = {QW: 160, HEAD: 48}


def mm(a, b):
    return lax.dot_general(a, b, (((1,), (0,)), ((), ())), preferred_element_type=F32)


def mm_nt(a, b):
    return lax.dot_general(a, b, (((1,), (1,)), ((), ())), preferred_element_type=F32)


def standardize(rows):
    centered = rows - jnp.mean(rows, axis=-1, keepdims=True)
    inverse_deviation = lax.rsqrt(jnp.mean(centered * centered, axis=-1, keepdims=True) + EPS)
    return centered * inverse_deviation, inverse_deviation


def kernel(
    x_hbm, wq_raw_hbm, wo_raw_hbm, up_hbm,
    hid_out, gq_out, go_out,
    wq_raw, wo_raw, wq_own, wo_own, wq, wo, nrm, up, xbuf, xrow, acc_q, acc_o, qkv, probs, rows_t, rows, rows_other, ctx_t,
    gq, go,
    q_ya, q_xa1, q_xa2, q_xb1, q_xb2, q_yb,
    o_ya, o_xa1, o_xa2, o_xb1, o_xb2, o_yb,
    sq_send, sq_recv, so_send, so_recv,
    gn, zr0, zr1, ysend, yrecv, gnf, xhat, inv,
    local_sem, send_sem, recv_sem,
):
    dp = lax.axis_index("dp")
    tn = lax.axis_index("tensor")
    core = lax.rem(dp, 2)
    other = 1 - core
    x = lax.rem(lax.div(dp, 2), 4)
    y = lax.div(dp, 8)
    z = lax.rem(tn, 8)
    yh = lax.div(tn, 8)

    def dp_at(yy, xx, cc):
        return (yy * 4 + xx) * 2 + cc

    sib = (dp_at(y, x, other), tn)
    xp = (dp_at(y, lax.rem(x + 1, 4), core), tn)
    xm = (dp_at(y, lax.rem(x + 3, 4), core), tn)
    yp = (dp_at(1 - y, x, core), tn)
    zp = (dp, yh * 8 + lax.rem(z + 1, 8))
    zm = (dp, yh * 8 + lax.rem(z + 7, 8))
    yhp = (dp, (1 - yh) * 8 + z)
    partners = (sib, xp, xm, yp, zp, zm, yhp)

    messages = []

    def send(src, dst, target):
        k = len(messages)
        copy = pltpu.make_async_remote_copy(
            src_ref=src, dst_ref=dst, send_sem=send_sem.at[k], recv_sem=recv_sem.at[k],
            device_id=target, device_id_type=MESH,
        )
        copy.start()
        messages.append(copy)
        return copy

    def chip_cols(slot):
        dy, dx = slot // 4, slot % 4
        chip = lax.rem(y + dy, 2) * 4 + lax.rem(x + dx, 4)
        return pl.ds(pl.multiple_of(chip * CHIP_D, 128), CHIP_D)

    def add_rows(n_rows, dst, *srcs):
        def body(r, carry):
            at = pl.ds(pl.multiple_of(r * 16, 16), 16)
            total = dst(at)[...].astype(F32)
            for src in srcs:
                total = total + src(at)[...].astype(F32)
            dst(at)[...] = total.astype(BF16)
            return carry

        lax.fori_loop(0, n_rows // 16, body, 0)

    barrier = pltpu.get_barrier_semaphore()
    for partner in partners:
        pl.semaphore_signal(barrier, inc=1, device_id=partner, device_id_type=MESH)
    token0 = pl.multiple_of(tn * 16, 16)
    loads = [
        pltpu.make_async_copy(x_hbm, xbuf, local_sem.at[0]),
        pltpu.make_async_copy(x_hbm.at[pl.ds(token0, 16)], xrow, local_sem.at[1]),
        pltpu.make_async_copy(wq_raw_hbm, wq_raw, local_sem.at[2]),
        pltpu.make_async_copy(wo_raw_hbm, wo_raw, local_sem.at[3]),
        pltpu.make_async_copy(up_hbm, up.at[0], local_sem.at[4]),
    ]
    for n in (2, 3, 0, 1):
        loads[n].start()
    loads[2].wait()
    for h in range(2):
        wq_own[h] = wq_raw[:, h, :]
    loads[3].wait()
    for h in range(2):
        wo_own[h] = wo_raw[:, h, :]
    own_loads = [
        pltpu.make_async_copy(wq_own.at[core], wq.at[0, core, :, pl.ds(0, QW)], local_sem.at[2]),
        pltpu.make_async_copy(wo_own.at[core], wo.at[0, core], local_sem.at[3]),
    ]
    for load in own_loads:
        load.start()
    pl.semaphore_wait(barrier, len(partners))

    A = pl.ds(0, GATHER_A)
    A0 = pl.ds(0, GATHER_A0)
    A1 = pl.ds(GATHER_A0, GATHER_A - GATHER_A0)
    B = pl.ds(GATHER_A, ROWS - GATHER_A)
    B0 = pl.ds(GATHER_A, GATHER_B0)
    B1 = pl.ds(GATHER_A + GATHER_B0, ROWS - GATHER_A - GATHER_B0)

    class Gather:
        def __init__(self, w, own, load, width):
            self.w, self.own, self.load, self.lanes = w, own, load, pl.ds(0, width)

        def at(self, slot, rows, part=slice(None)):
            return self.w.at[slot, part, rows, self.lanes]

        def move(self, slot, rows, to_slot, target):
            return send(self.at(slot, rows), self.at(to_slot, rows), target)

        def stage0(self):
            src = self.own
            self.swap = send(src.at[other], self.at(0, slice(None), core), sib)
            self.xa_p = [send(src.at[core, A], self.at(3, A, core), xp)]
            self.xa_m = [send(src.at[core, A], self.at(1, A, core), xm)]
            self.yb = [send(src.at[core, B], self.at(4, B, core), yp)]

        def stage0b(self):
            self.swap.wait_recv()
            self.xa_p.append(send(self.at(0, A, other), self.at(3, A, other), xp))
            self.xa_m.append(send(self.at(0, A, other), self.at(1, A, other), xm))
            self.yb.append(send(self.at(0, B, other), self.at(4, B, other), yp))
            self.load.wait()
            self.xb_p = self.move(0, B, 3, xp)
            self.xb_m = self.move(0, B, 1, xm)
            self.ya0 = self.move(0, A, 4, yp)

        def stage1(self):
            for m in self.xa_p:
                m.wait_recv()
            self.xa2_p = self.move(3, A0, 2, xp)
            for m in self.xa_m:
                m.wait_recv()
            self.xa2_m = self.move(1, A1, 2, xm)
            self.ya3 = self.move(3, A, 7, yp)
            self.ya1 = self.move(1, A, 5, yp)

        def stage2(self):
            for m in self.yb:
                m.wait_recv()
            self.xb3_p = self.move(4, B, 7, xp)
            self.xb3_m = self.move(4, B, 5, xm)

        def stage3(self):
            self.xb_p.wait_recv()
            self.xb2_p = self.move(3, B0, 2, xp)
            self.xb_m.wait_recv()
            self.xb2_m = self.move(1, B1, 2, xm)

        def stage4(self):
            self.xa2_p.wait_recv()
            self.ya2_p = self.move(2, A0, 6, yp)
            self.xa2_m.wait_recv()
            self.ya2_m = self.move(2, A1, 6, yp)

        def stage5(self):
            self.xb3_p.wait_recv()
            self.xb4_p = self.move(7, B0, 6, xp)
            self.xb3_m.wait_recv()
            self.xb4_m = self.move(5, B1, 6, xm)

        def complete(self, slot):
            pending = {
                0: (), 3: (), 1: (), 4: (self.ya0,),
                2: (self.xb2_p, self.xb2_m) if slot == 2 else (),
                7: (self.ya3,), 5: (self.ya1,),
                6: (self.ya2_p, self.ya2_m, self.xb4_p, self.xb4_m) if slot == 6 else (),
            }[slot]
            for m in pending:
                m.wait_recv()

    g_q = Gather(wq, wq_own, own_loads[0], QW)
    g_o = Gather(wo, wo_own, own_loads[1], HEAD)
    g_q.stage0()
    g_q.stage0b()

    loads[0].wait()

    def norm_rows(r, carry):
        at = pl.ds(pl.multiple_of(r * 16, 16), 16)
        standardized, _ = standardize(xbuf[at, :].astype(F32))
        nrm[0, at, :] = standardized.astype(BF16)
        return carry

    lax.fori_loop(0, SEQ // 16, norm_rows, 0)
    nrm_msg = send(nrm.at[0], nrm.at[1], sib)

    def project(acc, w, left, width, slot):
        a = left[:, :, chip_cols(slot)].reshape(2 * SEQ, CHIP_D)
        product = mm(a, w[slot, :, :, pl.ds(0, width)].reshape(CHIP_D, width))
        if slot == 0:
            acc[...] = product
        else:
            acc[...] += product

    share_msgs = []

    def project_q(slot):
        g_q.complete(slot)
        share_msgs.append(send(
            wq.at[slot, :, :, pl.ds(0, QW)], wq.at[slot, :, :, pl.ds(QW, QW)], sib
        ))
        project(acc_q, wq, nrm, QW, slot)

    def project_o(slot):
        g_o.complete(slot)
        project(acc_o, wo, up, HEAD, slot)

    g_q.stage1()
    g_q.stage2()
    loads[4].start()
    up_msg = send(up_hbm, up.at[1], sib)
    loads[1].wait()
    own_xhat, own_inv = standardize(xrow[...].astype(F32))
    xhat[...] = own_xhat
    inv[...] = jnp.broadcast_to(own_inv, (16, 128))
    nrm_msg.wait_recv()
    project_q(0)
    g_q.stage3()
    project_q(3)
    g_q.stage4()
    project_q(1)
    project_q(4)
    g_q.stage5()
    g_o.stage0()
    project_q(7)
    g_o.stage0b()
    project_q(5)
    project_q(2)
    project_q(6)
    qkv[...] = acc_q[...].astype(BF16)

    scale = 1.0 / math.sqrt(HEAD)

    def forward(s):
        at = pl.ds(s * SEQ, SEQ)
        query, key, value = (qkv[at, pl.ds(n * HEAD, HEAD)] for n in range(3))
        raised = jnp.exp(mm_nt(query, key) * scale)
        attn = raised / jnp.sum(raised, axis=-1, keepdims=True)
        probs[s] = attn
        context = mm(attn.astype(BF16), value).astype(BF16).astype(F32)
        ctx_t[:, at] = context.T.astype(BF16)

    loads[4].wait()
    up_msg.wait_recv()
    forward(0)
    g_o.stage1()
    forward(1)
    g_o.stage2()
    project_o(0)


    def weight_unit(g, left_t, right, slot):
        b = right[:, :, chip_cols(slot)].reshape(2 * SEQ, CHIP_D)
        g[slot] = mm(left_t[...], b).astype(BF16)

    L = (pl.ds(0, ROWS), pl.ds(ROWS, ROWS))

    class Scatter:
        def __init__(self, g, width, ya, xa1, xa2, xb1, xb2, yb):
            self.g, self.width = g, width
            self.na = SCATTER_A[width]
            self.nb = width - self.na
            self.A, self.B = pl.ds(0, self.na), pl.ds(self.na, self.nb)
            self.ya, self.xa1, self.xa2, self.xb1, self.xb2, self.yb = ya, xa1, xa2, xb1, xb2, yb
            self.m = {}

        def rows_a(self, slot, lanes=slice(None)):
            return lambda at: self.g.at[slot, at, lanes]

        def rows_b(self, slot, lanes=slice(None)):
            def view(at):
                return self.g.at[slot, pl.ds(pl.multiple_of(at.start + self.na, 16), 16), lanes]

            return view

        def send_ya(self, dx):
            self.m["ya", dx] = send(self.g.at[4 + dx, self.A], self.ya.at[dx], yp)

        def send_xb1(self, dy):
            for n, target in enumerate((xp, xm)):
                self.m["xb1", dy, n] = send(
                    self.g.at[dy * 4 + 2, self.B, L[n]], self.xb1.at[dy, n], target
                )

        def step_xb2(self, dy):
            for n, (slot, target) in enumerate(((1, xp), (3, xm))):
                self.m["xb1", dy, n].wait_recv()
                add_rows(
                    self.nb, self.rows_b(dy * 4 + slot, L[n]),
                    lambda at, n=n: self.xb1.at[dy, n, at],
                )
                self.m["xb2", dy, n] = send(
                    self.g.at[dy * 4 + slot, self.B], self.xb2.at[dy, n], target
                )

        def step_xa1(self):
            self.m["ya", 2].wait_recv()
            add_rows(self.na, self.rows_a(2), lambda at: self.ya.at[2, at])
            for n, target in enumerate((xp, xm)):
                self.m["xa1", n] = send(self.g.at[2, self.A, L[n]], self.xa1.at[n], target)

        def step_xa2(self):
            for n, (slot, target) in enumerate(((1, xp), (3, xm))):
                self.m["ya", slot].wait_recv()
                self.m["xa1", n].wait_recv()
                add_rows(
                    self.na, self.rows_a(slot, L[n]),
                    lambda at, n=n, slot=slot: self.ya.at[slot, at, L[n]],
                    lambda at, n=n: self.xa1.at[n, at],
                )
                add_rows(
                    self.na, self.rows_a(slot, L[1 - n]),
                    lambda at, n=n, slot=slot: self.ya.at[slot, at, L[1 - n]],
                )
                self.m["xa2", n] = send(self.g.at[slot, self.A], self.xa2.at[n], target)

        def step_yb(self):
            for n in range(2):
                self.m["xb2", 1, n].wait_recv()
            add_rows(
                self.nb, self.rows_b(4),
                lambda at: self.xb2.at[1, 0, at], lambda at: self.xb2.at[1, 1, at],
            )
            self.m["yb"] = send(self.g.at[4, self.B], self.yb, yp)

        def finish(self, out, send_buf, recv_buf):
            for key in (("xb2", 0, 0), ("xb2", 0, 1), ("ya", 0), ("xa2", 0), ("xa2", 1), "yb"):
                self.m[key].wait_recv()

            def total(lanes):
                a = self.g[0, self.A, lanes].astype(F32) + self.ya[0, :, lanes].astype(F32)
                a = a + self.xa2[0, :, lanes].astype(F32) + self.xa2[1, :, lanes].astype(F32)
                b = self.g[0, self.B, lanes].astype(F32) + self.yb[:, lanes].astype(F32)
                b = b + self.xb2[0, 0, :, lanes].astype(F32) + self.xb2[0, 1, :, lanes].astype(F32)
                return jnp.concatenate([a, b], axis=0) * (1.0 / N_DP)

            def lanes_of(cc):
                return pl.ds(pl.multiple_of(cc * ROWS, 128), ROWS)

            send_buf[...] = total(lanes_of(other)).astype(BF16)
            message = send(send_buf, recv_buf, sib)

            def write(value, head):
                for h in range(2):
                    pl.when(head == h)(lambda h=h: write_at(value, h))

            def write_at(value, head):
                for fb in range(self.width // HEAD):
                    out[:, head, pl.ds(fb * HEAD, HEAD)] = value[fb * HEAD:(fb + 1) * HEAD, :].T

            write(total(lanes_of(core)), core)
            message.wait_recv()
            write(recv_buf[...].astype(F32), other)

    s_o = Scatter(go, HEAD, o_ya, o_xa1, o_xa2, o_xb1, o_xb2, o_yb)
    s_q = Scatter(gq, QW, q_ya, q_xa1, q_xa2, q_xb1, q_xb2, q_yb)

    def o_units(*slots):
        for slot in slots:
            weight_unit(go, ctx_t, up, slot)

    g_o.stage3()
    g_o.stage4()
    o_units(6, 2)
    project_o(3)
    s_o.send_xb1(1)
    s_o.send_xb1(0)
    s_o.send_ya(2)
    g_o.stage5()
    o_units(5, 7)
    s_o.send_ya(1)
    s_o.send_ya(3)
    project_o(1)
    project_o(4)
    o_units(4)
    s_o.send_ya(0)
    o_units(1, 3, 0)
    project_o(7)
    project_o(5)
    project_o(2)
    project_o(6)

    def backward(s):
        at = pl.ds(s * SEQ, SEQ)
        query, key, value = (qkv[at, pl.ds(n * HEAD, HEAD)] for n in range(3))
        grad_context = acc_o[at, :].astype(BF16)
        attn = probs[s]
        grad_prob = mm_nt(grad_context, value)
        row_dot = jnp.sum(attn * grad_prob, axis=-1, keepdims=True)
        grad_score = (attn * (grad_prob - row_dot) * scale).astype(BF16)
        query_t = query.astype(F32).T.astype(BF16)
        key_t = key.astype(F32).T.astype(BF16)
        grad_context_t = grad_context.astype(F32).T.astype(BF16)
        parts = (
            mm_nt(key_t, grad_score),
            mm(query_t, grad_score),
            mm(grad_context_t, attn.astype(BF16)),
        )
        for n, part in enumerate(parts):
            rows_t[pl.ds(n * HEAD, HEAD), at] = part.astype(BF16)
            lanes = pl.ds(n * HEAD, HEAD)
            if s == 0:
                rows[:, lanes] = part.T.astype(BF16)
            else:
                rows_other[:, lanes] = part.T.astype(BF16)

    s_o.step_xb2(1)
    backward(1)
    rows_msg = send(rows_other, rows.at[:, pl.ds(QW, QW)], sib)
    s_o.step_xb2(0)
    backward(0)

    def gn_group(g):
        for slot in (2 * g, 2 * g + 1):
            share_msgs[SLOT_ORDER.index(slot)].wait_recv()
            part = mm_nt(rows[...], wq[slot].reshape(CHIP_D, 2 * QW)).astype(BF16)
            gn[slot] = part.reshape(2, 128, CHIP_D)
        gn_step0(g)

    def z_rows(dz):
        return pl.ds(pl.multiple_of(lax.rem(z + dz + 8, 8) * 16, 16), 16)

    zm_msgs = {}
    directions = ((zp, 1), (zm, -1))

    def gn_step0(g):
        for n, (target, _) in enumerate(directions):
            zm_msgs[g, 0, n] = send(gn.at[2 * g + n, :, z_rows(4)], zr0.at[n, g], target)

    def gn_step(g, step):
        for n, (target, sign) in enumerate(directions):
            at = z_rows(sign * (4 - step))
            zm_msgs[g, step - 1, n].wait_recv()
            if step == 1:
                mine = gn[2 * g + n, :, at, :].astype(F32)
                gn[2 * g + n, :, at, :] = (mine + zr0[n, g].astype(F32)).astype(BF16)
            else:
                mine = gn[pl.ds(2 * g, 2), :, at, :].astype(F32)
                mine = mine + zr1[n, g, step - 2].astype(F32)
                gn[pl.ds(2 * g, 2), :, at, :] = mine.astype(BF16)
            zm_msgs[g, step, n] = send(
                gn.at[pl.ds(2 * g, 2), :, at], zr1.at[n, g, step - 1], target
            )

    def gn_sum(g, which):
        at = z_rows(0)
        pair = pl.ds(2 * g, 2)
        total = gn[pair, which, at, :].astype(F32)
        return total + zr1[0, g, 2, :, which].astype(F32) + zr1[1, g, 2, :, which].astype(F32)

    def gn_exchange(g):
        for n in range(2):
            zm_msgs[g, 3, n].wait_recv()
        ysend[g] = gn_sum(g, 1 - yh).astype(BF16)
        zm_msgs[g, "y"] = send(ysend.at[g], yrecv.at[g], yhp)

    def gn_finish(g):
        zm_msgs[g, "y"].wait_recv()
        total = gn_sum(g, yh) + yrecv[g].astype(F32)
        for n in range(2):
            gnf[:, chip_cols(2 * g + n)] = total[n]

    def q_units(*slots):
        for slot in slots:
            weight_unit(gq, rows_t, nrm, slot)

    q_units(6)
    s_q.send_xb1(1)
    s_q.send_ya(2)
    rows_msg.wait_recv()
    gn_group(0)
    q_units(2)
    s_q.send_xb1(0)
    gn_group(1)
    s_o.step_xa1()
    gn_step(0, 1)
    q_units(5, 7)
    s_q.send_ya(1)
    s_q.send_ya(3)
    gn_group(2)
    gn_step(1, 1)
    gn_step(0, 2)
    q_units(1, 3)
    s_q.step_xb2(1)
    s_q.step_xa1()
    gn_group(3)
    gn_step(2, 1)
    gn_step(1, 2)
    q_units(4)
    s_q.send_ya(0)
    s_o.step_yb()
    gn_step(0, 3)
    gn_step(3, 1)
    s_o.step_xa2()
    gn_step(2, 2)
    q_units(0)
    gn_step(1, 3)
    s_q.step_yb()
    s_q.step_xa2()
    gn_exchange(0)
    gn_step(3, 2)
    s_q.step_xb2(0)
    gn_step(2, 3)
    gn_exchange(1)
    gn_step(3, 3)
    s_o.finish(go_out, so_send, so_recv)
    gn_exchange(2)
    gn_exchange(3)
    for g in range(GROUPS):
        gn_finish(g)
    s_q.finish(gq_out, sq_send, sq_recv)

    total = gnf[...]
    standardized = xhat[...]
    mean_g = jnp.mean(total, axis=-1, keepdims=True)
    mean_p = jnp.mean(total * standardized, axis=-1, keepdims=True)
    hid_out[...] = (inv[:, :1] * (total - mean_g - standardized * mean_p)).astype(BF16)

    for message in messages:
        message.wait_send()


def scatter_buffers(width):
    a = SCATTER_A[width]
    b = width - a
    return [
        pltpu.VMEM((4, a, CHIP_D), BF16),
        pltpu.VMEM((2, a, ROWS), BF16),
        pltpu.VMEM((2, a, CHIP_D), BF16),
        pltpu.VMEM((2, 2, b, ROWS), BF16),
        pltpu.VMEM((2, 2, b, CHIP_D), BF16),
        pltpu.VMEM((b, CHIP_D), BF16),
    ]


def hand_over_kernel(*refs):
    sources, targets, held, sem = refs[:3], refs[3:6], refs[6:9], refs[9]
    loads, stores = (
        [pltpu.make_async_copy(a, b, sem.at[k, n]) for n, (a, b) in enumerate(zip(froms, tos))]
        for k, (froms, tos) in enumerate(((sources, held), (held, targets)))
    )
    for load in loads:
        load.start()
    for load, store in zip(loads, stores):
        load.wait()
        store.start()
    for store in stores:
        store.wait()


def hand_over(*arrays):
    any_spec = pl.BlockSpec(memory_space=pl.ANY)
    return pl.pallas_call(
        hand_over_kernel,
        out_shape=tuple(jax.ShapeDtypeStruct(a.shape, a.dtype) for a in arrays),
        in_specs=[any_spec] * 3,
        out_specs=(any_spec,) * 3,
        scratch_shapes=[pltpu.VMEM(a.shape, a.dtype) for a in arrays]
        + [pltpu.SemaphoreType.DMA((2, 3))],
    )(*arrays)


def per_device(sublayer_input, w_qkv, w_out, upstream_grad):
    scratch = [
        pltpu.VMEM((ROWS, 2, QW), BF16),
        pltpu.VMEM((ROWS, 2, HEAD), BF16),
        pltpu.VMEM((2, ROWS, QW), BF16),
        pltpu.VMEM((2, ROWS, HEAD), BF16),
        pltpu.VMEM((N_CHIPS, 2, ROWS, 2 * QW), BF16),
        pltpu.VMEM((N_CHIPS, 2, ROWS, HEAD), BF16),
        pltpu.VMEM((2, SEQ, D), BF16),
        pltpu.VMEM((2, SEQ, D), BF16),
        pltpu.VMEM((SEQ, D), BF16),
        pltpu.VMEM((16, D), BF16),
        pltpu.VMEM((2 * SEQ, QW), F32),
        pltpu.VMEM((2 * SEQ, HEAD), F32),
        pltpu.VMEM((2 * SEQ, QW), BF16),
        pltpu.VMEM((2, SEQ, SEQ), F32),
        pltpu.VMEM((QW, 2 * SEQ), BF16),
        pltpu.VMEM((SEQ, 2 * QW), BF16),
        pltpu.VMEM((SEQ, QW), BF16),
        pltpu.VMEM((HEAD, 2 * SEQ), BF16),
        pltpu.VMEM((N_CHIPS, QW, CHIP_D), BF16),
        pltpu.VMEM((N_CHIPS, HEAD, CHIP_D), BF16),
        *scatter_buffers(QW),
        *scatter_buffers(HEAD),
        pltpu.VMEM((QW, ROWS), BF16),
        pltpu.VMEM((QW, ROWS), BF16),
        pltpu.VMEM((HEAD, ROWS), BF16),
        pltpu.VMEM((HEAD, ROWS), BF16),
        pltpu.VMEM((N_CHIPS, 2, 128, CHIP_D), BF16),
        pltpu.VMEM((2, GROUPS, 2, 16, CHIP_D), BF16),
        pltpu.VMEM((2, GROUPS, 3, 2, 2, 16, CHIP_D), BF16),
        pltpu.VMEM((GROUPS, 2, 16, CHIP_D), BF16),
        pltpu.VMEM((GROUPS, 2, 16, CHIP_D), BF16),
        pltpu.VMEM((16, D), F32),
        pltpu.VMEM((16, D), F32),
        pltpu.VMEM((16, 128), F32),
        pltpu.SemaphoreType.DMA((5,)),
        pltpu.SemaphoreType.DMA((N_MESSAGES,)),
        pltpu.SemaphoreType.DMA((N_MESSAGES,)),
    ]
    any_spec = pl.BlockSpec(memory_space=pl.ANY)
    vmem_spec = pl.BlockSpec(memory_space=pltpu.VMEM)
    hid, gq, go = pl.pallas_call(
        kernel,
        out_shape=(
            jax.ShapeDtypeStruct((16, D), BF16),
            jax.ShapeDtypeStruct((ROWS, 2, QW), F32),
            jax.ShapeDtypeStruct((ROWS, 2, HEAD), F32),
        ),
        in_specs=[any_spec] * 4,
        out_specs=(vmem_spec,) * 3,
        scratch_shapes=scratch,
        compiler_params=pltpu.CompilerParams(
            collective_id=0, has_side_effects=True, vmem_limit_bytes=62 * 2**20
        ),
        cost_estimate=pl.CostEstimate(
            flops=10_000_000_000, bytes_accessed=10_000_000, transcendentals=200_000
        ),
    )(sublayer_input, w_qkv, w_out, upstream_grad)
    return hand_over(hid, gq, go)


def solution(mesh):
    in_specs = (P("dp", None), P("dp", "tensor", None), P("dp", "tensor", None), P("dp", None))
    out_specs = (P(("dp", "tensor"), None), P("dp", "tensor", None), P("dp", "tensor", None))
    return jax.shard_map(
        per_device, mesh=mesh, in_specs=in_specs, out_specs=out_specs, check_vma=False
    )
```

```python
import math

import jax
import jax.numpy as jnp
from jax import lax
from jax.experimental import pallas as pl
from jax.experimental.pallas import tpu as pltpu
from jax.sharding import PartitionSpec as P

EPS = 1e-05
MESH = pl.DeviceIdType.MESH
BF16 = jnp.bfloat16
F32 = jnp.float32

D = 6144
ROWS = 384
SEQ = 256
HEAD = 128
CHIP_D = 2 * ROWS
QW = 3 * HEAD
N_CHIPS = 8
N_DP = 16
GROUPS = 4
N_MESSAGES = 200
SLOT_ORDER = (0, 3, 1, 4, 7, 5, 2, 6)

GATHER_A, GATHER_A0, GATHER_B0 = 160, 80, 112
SCATTER_A = {QW: 160, HEAD: 48}


def mm(a, b):
    return lax.dot_general(a, b, (((1,), (0,)), ((), ())), preferred_element_type=F32)


def mm_nt(a, b):
    return lax.dot_general(a, b, (((1,), (1,)), ((), ())), preferred_element_type=F32)


def standardize(rows):
    centered = rows - jnp.mean(rows, axis=-1, keepdims=True)
    inverse_deviation = lax.rsqrt(jnp.mean(centered * centered, axis=-1, keepdims=True) + EPS)
    return centered * inverse_deviation, inverse_deviation


def kernel(
    x_hbm, wq_raw_hbm, wo_raw_hbm, up_hbm,
    hid_out, gq_out, go_out,
    wq_raw, wo_raw, wq_own, wo_own, wq, wo, nrm, up, xbuf, xrow, acc_q, acc_o, qkv, probs, rows_t, rows, rows_other, ctx_t,
    gq, go,
    q_ya, q_xa1, q_xb1, q_xb2, q_own, q_last_ya, q_last_xa, q_last_yb, q_last_xb, q_sum_a,
    o_ya, o_xa1, o_xb1, o_xb2, o_own, o_last_ya, o_last_xa, o_last_yb, o_last_xb, o_sum_a,
    gn, zr0, zr1, ysend, yrecv, gnf, xhat, inv,
    local_sem, send_sem, recv_sem,
):
    dp = lax.axis_index("dp")
    tn = lax.axis_index("tensor")
    core = lax.rem(dp, 2)
    other = 1 - core
    x = lax.rem(lax.div(dp, 2), 4)
    y = lax.div(dp, 8)
    z = lax.rem(tn, 8)
    yh = lax.div(tn, 8)

    def dp_at(yy, xx, cc):
        return (yy * 4 + xx) * 2 + cc

    sib = (dp_at(y, x, other), tn)
    xp = (dp_at(y, lax.rem(x + 1, 4), core), tn)
    xm = (dp_at(y, lax.rem(x + 3, 4), core), tn)
    yp = (dp_at(1 - y, x, core), tn)
    zp = (dp, yh * 8 + lax.rem(z + 1, 8))
    zm = (dp, yh * 8 + lax.rem(z + 7, 8))
    yhp = (dp, (1 - yh) * 8 + z)
    xp_other = (dp_at(y, lax.rem(x + 1, 4), other), tn)
    xm_other = (dp_at(y, lax.rem(x + 3, 4), other), tn)
    yp_other = (dp_at(1 - y, x, other), tn)
    partners = (sib, xp, xm, yp, zp, zm, yhp, xp_other, xm_other, yp_other)

    messages = []

    def send(src, dst, target):
        k = len(messages)
        copy = pltpu.make_async_remote_copy(
            src_ref=src, dst_ref=dst, send_sem=send_sem.at[k], recv_sem=recv_sem.at[k],
            device_id=target, device_id_type=MESH,
        )
        copy.start()
        messages.append(copy)
        return copy

    def chip_cols(slot):
        dy, dx = slot // 4, slot % 4
        chip = lax.rem(y + dy, 2) * 4 + lax.rem(x + dx, 4)
        return pl.ds(pl.multiple_of(chip * CHIP_D, 128), CHIP_D)

    def add_rows(n_rows, dst, *srcs):
        def body(r, carry):
            at = pl.ds(pl.multiple_of(r * 16, 16), 16)
            total = dst(at)[...].astype(F32)
            for src in srcs:
                total = total + src(at)[...].astype(F32)
            dst(at)[...] = total.astype(BF16)
            return carry

        lax.fori_loop(0, n_rows // 16, body, 0)

    barrier = pltpu.get_barrier_semaphore()
    for partner in partners:
        pl.semaphore_signal(barrier, inc=1, device_id=partner, device_id_type=MESH)
    token0 = pl.multiple_of(tn * 16, 16)
    loads = [
        pltpu.make_async_copy(x_hbm, xbuf, local_sem.at[0]),
        pltpu.make_async_copy(x_hbm.at[pl.ds(token0, 16)], xrow, local_sem.at[1]),
        pltpu.make_async_copy(wq_raw_hbm, wq_raw, local_sem.at[2]),
        pltpu.make_async_copy(wo_raw_hbm, wo_raw, local_sem.at[3]),
        pltpu.make_async_copy(up_hbm, up.at[0], local_sem.at[4]),
    ]
    for n in (2, 3, 0, 1):
        loads[n].start()
    loads[2].wait()
    for h in range(2):
        wq_own[h] = wq_raw[:, h, :]
    loads[3].wait()
    for h in range(2):
        wo_own[h] = wo_raw[:, h, :]
    own_loads = [
        pltpu.make_async_copy(wq_own.at[core], wq.at[0, core, :, pl.ds(0, QW)], local_sem.at[2]),
        pltpu.make_async_copy(wo_own.at[core], wo.at[0, core], local_sem.at[3]),
    ]
    for load in own_loads:
        load.start()
    pl.semaphore_wait(barrier, len(partners))

    A = pl.ds(0, GATHER_A)
    A0 = pl.ds(0, GATHER_A0)
    A1 = pl.ds(GATHER_A0, GATHER_A - GATHER_A0)
    B = pl.ds(GATHER_A, ROWS - GATHER_A)
    B0 = pl.ds(GATHER_A, GATHER_B0)
    B1 = pl.ds(GATHER_A + GATHER_B0, ROWS - GATHER_A - GATHER_B0)

    class Gather:
        def __init__(self, w, own, load, width):
            self.w, self.own, self.load, self.lanes = w, own, load, pl.ds(0, width)

        def at(self, slot, rows, part=slice(None)):
            return self.w.at[slot, part, rows, self.lanes]

        def move(self, slot, rows, to_slot, target):
            return send(self.at(slot, rows), self.at(to_slot, rows), target)

        def stage0(self):
            src = self.own
            self.swap = send(src.at[other], self.at(0, slice(None), core), sib)
            self.xa_p = [send(src.at[core, A], self.at(3, A, core), xp)]
            self.xa_m = [send(src.at[core, A], self.at(1, A, core), xm)]
            self.yb = [send(src.at[core, B], self.at(4, B, core), yp)]

        def stage0b(self):
            self.swap.wait_recv()
            self.xa_p.append(send(self.at(0, A, other), self.at(3, A, other), xp))
            self.xa_m.append(send(self.at(0, A, other), self.at(1, A, other), xm))
            self.yb.append(send(self.at(0, B, other), self.at(4, B, other), yp))
            self.load.wait()
            self.xb_p = self.move(0, B, 3, xp)
            self.xb_m = self.move(0, B, 1, xm)
            self.ya0 = self.move(0, A, 4, yp)

        def stage1(self):
            for m in self.xa_p:
                m.wait_recv()
            self.xa2_p = self.move(3, A0, 2, xp)
            for m in self.xa_m:
                m.wait_recv()
            self.xa2_m = self.move(1, A1, 2, xm)
            self.ya3 = self.move(3, A, 7, yp)
            self.ya1 = self.move(1, A, 5, yp)

        def stage2(self):
            for m in self.yb:
                m.wait_recv()
            self.xb3_p = self.move(4, B, 7, xp)
            self.xb3_m = self.move(4, B, 5, xm)

        def stage3(self):
            self.xb_p.wait_recv()
            self.xb2_p = self.move(3, B0, 2, xp)
            self.xb_m.wait_recv()
            self.xb2_m = self.move(1, B1, 2, xm)

        def stage4(self):
            self.xa2_p.wait_recv()
            self.ya2_p = self.move(2, A0, 6, yp)
            self.xa2_m.wait_recv()
            self.ya2_m = self.move(2, A1, 6, yp)

        def stage5(self):
            self.xb3_p.wait_recv()
            self.xb4_p = self.move(7, B0, 6, xp)
            self.xb3_m.wait_recv()
            self.xb4_m = self.move(5, B1, 6, xm)

        def complete(self, slot):
            pending = {
                0: (), 3: (), 1: (), 4: (self.ya0,),
                2: (self.xb2_p, self.xb2_m) if slot == 2 else (),
                7: (self.ya3,), 5: (self.ya1,),
                6: (self.ya2_p, self.ya2_m, self.xb4_p, self.xb4_m) if slot == 6 else (),
            }[slot]
            for m in pending:
                m.wait_recv()

    g_q = Gather(wq, wq_own, own_loads[0], QW)
    g_o = Gather(wo, wo_own, own_loads[1], HEAD)
    g_q.stage0()
    g_q.stage0b()

    loads[0].wait()

    def norm_rows(r, carry):
        at = pl.ds(pl.multiple_of(r * 16, 16), 16)
        standardized, _ = standardize(xbuf[at, :].astype(F32))
        nrm[0, at, :] = standardized.astype(BF16)
        return carry

    lax.fori_loop(0, SEQ // 16, norm_rows, 0)
    nrm_msg = send(nrm.at[0], nrm.at[1], sib)

    def project(acc, w, left, width, slot):
        a = left[:, :, chip_cols(slot)].reshape(2 * SEQ, CHIP_D)
        product = mm(a, w[slot, :, :, pl.ds(0, width)].reshape(CHIP_D, width))
        if slot == 0:
            acc[...] = product
        else:
            acc[...] += product

    share_msgs = []

    def project_q(slot):
        g_q.complete(slot)
        share_msgs.append(send(
            wq.at[slot, :, :, pl.ds(0, QW)], wq.at[slot, :, :, pl.ds(QW, QW)], sib
        ))
        project(acc_q, wq, nrm, QW, slot)

    def project_o(slot):
        g_o.complete(slot)
        project(acc_o, wo, up, HEAD, slot)

    g_q.stage1()
    g_q.stage2()
    loads[4].start()
    up_msg = send(up_hbm, up.at[1], sib)
    loads[1].wait()
    own_xhat, own_inv = standardize(xrow[...].astype(F32))
    xhat[...] = own_xhat
    inv[...] = jnp.broadcast_to(own_inv, (16, 128))
    nrm_msg.wait_recv()
    project_q(0)
    g_q.stage3()
    project_q(3)
    g_q.stage4()
    project_q(1)
    project_q(4)
    g_q.stage5()
    g_o.stage0()
    project_q(7)
    g_o.stage0b()
    project_q(5)
    project_q(2)
    project_q(6)
    qkv[...] = acc_q[...].astype(BF16)

    scale = 1.0 / math.sqrt(HEAD)

    def forward(s):
        at = pl.ds(s * SEQ, SEQ)
        query, key, value = (qkv[at, pl.ds(n * HEAD, HEAD)] for n in range(3))
        raised = jnp.exp(mm_nt(query, key) * scale)
        attn = raised / jnp.sum(raised, axis=-1, keepdims=True)
        probs[s] = attn
        context = mm(attn.astype(BF16), value).astype(BF16).astype(F32)
        ctx_t[:, at] = context.T.astype(BF16)

    def weight_unit(g, left_t, right, slot):
        b = right[:, :, chip_cols(slot)].reshape(2 * SEQ, CHIP_D)
        g[slot] = mm(left_t[...], b).astype(BF16)

    L = (pl.ds(0, ROWS), pl.ds(ROWS, ROWS))

    def lanes_of(cc):
        return pl.ds(pl.multiple_of(cc * ROWS, 128), ROWS)

    class Scatter:
        def __init__(
            self, g, width, ya, xa1, xb1, xb2, own, last_ya, last_xa, last_yb, last_xb, sum_a
        ):
            self.g, self.width = g, width
            self.na = SCATTER_A[width]
            self.nb = width - self.na
            self.A, self.B = pl.ds(0, self.na), pl.ds(self.na, self.nb)
            self.ya, self.xa1, self.xb1, self.xb2, self.own = ya, xa1, xb1, xb2, own
            self.last_ya, self.last_xa, self.last_yb, self.last_xb = last_ya, last_xa, last_yb, last_xb
            self.sum_a = sum_a
            self.m = {}

        def rows_a(self, slot, lanes=slice(None)):
            return lambda at: self.g.at[slot, at, lanes]

        def rows_b(self, slot, lanes=slice(None)):
            def view(at):
                return self.g.at[slot, pl.ds(pl.multiple_of(at.start + self.na, 16), 16), lanes]

            return view

        def last_hop(self, slot, rows, buf, target, target_other):
            return [
                send(self.g.at[slot, rows, lanes_of(cc)], buf.at[core], to)
                for cc, to in ((core, target), (other, target_other))
            ]

        def send_own(self):
            self.m["own"] = [send(self.g.at[0, :, lanes_of(other)], self.own, sib)]

        def send_ya(self, dx):
            if dx == 0:
                self.m["ya", 0] = self.last_hop(4, self.A, self.last_ya, yp, yp_other)
            else:
                self.m["ya", dx] = send(self.g.at[4 + dx, self.A], self.ya.at[dx - 1], yp)

        def send_xb1(self, dy):
            for n, target in enumerate((xp, xm)):
                self.m["xb1", dy, n] = send(
                    self.g.at[dy * 4 + 2, self.B, L[n]], self.xb1.at[dy, n], target
                )

        def step_xb2(self, dy):
            for n, (slot, target, target_other) in enumerate(((1, xp, xp_other), (3, xm, xm_other))):
                self.m["xb1", dy, n].wait_recv()
                at_slot = dy * 4 + slot
                add_rows(
                    self.nb, self.rows_b(at_slot, L[n]), lambda at, n=n: self.xb1.at[dy, n, at]
                )
                if dy == 0:
                    self.m["xb2", 0, n] = self.last_hop(
                        at_slot, self.B, self.last_xb.at[n], target, target_other
                    )
                else:
                    self.m["xb2", 1, n] = send(self.g.at[at_slot, self.B], self.xb2.at[n], target)

        def step_xa1(self):
            self.m["ya", 2].wait_recv()
            add_rows(self.na, self.rows_a(2), lambda at: self.ya.at[1, at])
            for n, target in enumerate((xp, xm)):
                self.m["xa1", n] = send(self.g.at[2, self.A, L[n]], self.xa1.at[n], target)

        def step_xa2(self):
            for n, (slot, target, target_other) in enumerate(((1, xp, xp_other), (3, xm, xm_other))):
                self.m["ya", slot].wait_recv()
                self.m["xa1", n].wait_recv()
                add_rows(
                    self.na, self.rows_a(slot, L[n]),
                    lambda at, n=n, slot=slot: self.ya.at[slot - 1, at, L[n]],
                    lambda at, n=n: self.xa1.at[n, at],
                )
                add_rows(
                    self.na, self.rows_a(slot, L[1 - n]),
                    lambda at, n=n, slot=slot: self.ya.at[slot - 1, at, L[1 - n]],
                )
                self.m["xa2", n] = self.last_hop(
                    slot, self.A, self.last_xa.at[n], target, target_other
                )

        def step_yb(self):
            for n in range(2):
                self.m["xb2", 1, n].wait_recv()
            add_rows(
                self.nb, self.rows_b(4),
                lambda at: self.xb2.at[0, at], lambda at: self.xb2.at[1, at],
            )
            self.m["yb"] = self.last_hop(4, self.B, self.last_yb, yp, yp_other)

        def total(self, rows, h, *received):
            mine = self.g[0, rows, lanes_of(core)].astype(F32)
            total = jnp.where(core == h, mine, self.own[rows, :].astype(F32))
            for part in received:
                total = total + part.astype(F32)
            return total * (1.0 / N_DP)

        def wait_last(self, *keys):
            for key in keys:
                for message in self.m[key]:
                    message.wait_recv()

        def write(self, out, value, fb, h):
            out[:, h, pl.ds(fb * HEAD, HEAD)] = value.T

        def finish_a(self, out):
            self.wait_last("own", ("ya", 0), ("xa2", 0), ("xa2", 1))
            for h in range(2):
                total = self.total(
                    self.A, h, self.last_ya[h], self.last_xa[0, h], self.last_xa[1, h]
                )
                self.sum_a[h] = total
                if self.na >= HEAD:
                    self.write(out, total[:HEAD], 0, h)

        def finish_b(self, out):
            self.wait_last(("xb2", 0, 0), ("xb2", 0, 1), "yb")
            done = self.na // HEAD
            for h in range(2):
                total = self.total(
                    self.B, h, self.last_yb[h], self.last_xb[0, h], self.last_xb[1, h]
                )
                rest = jnp.concatenate([self.sum_a[h, done * HEAD:, :], total], axis=0)
                for fb in range(done, self.width // HEAD):
                    at = (fb - done) * HEAD
                    self.write(out, rest[at:at + HEAD], fb, h)

    s_o = Scatter(
        go, HEAD, o_ya, o_xa1, o_xb1, o_xb2, o_own,
        o_last_ya, o_last_xa, o_last_yb, o_last_xb, o_sum_a,
    )
    s_q = Scatter(
        gq, QW, q_ya, q_xa1, q_xb1, q_xb2, q_own,
        q_last_ya, q_last_xa, q_last_yb, q_last_xb, q_sum_a,
    )

    def o_units(slot):
        weight_unit(go, ctx_t, up, slot)

    def backward(s):
        at = pl.ds(s * SEQ, SEQ)
        query, key, value = (qkv[at, pl.ds(n * HEAD, HEAD)] for n in range(3))
        grad_context = acc_o[at, :].astype(BF16)
        attn = probs[s]
        grad_prob = mm_nt(grad_context, value)
        row_dot = jnp.sum(attn * grad_prob, axis=-1, keepdims=True)
        grad_score = (attn * (grad_prob - row_dot) * scale).astype(BF16)
        query_t = query.astype(F32).T.astype(BF16)
        key_t = key.astype(F32).T.astype(BF16)
        grad_context_t = grad_context.astype(F32).T.astype(BF16)
        parts = (
            mm_nt(key_t, grad_score),
            mm(query_t, grad_score),
            mm(grad_context_t, attn.astype(BF16)),
        )
        for n, part in enumerate(parts):
            rows_t[pl.ds(n * HEAD, HEAD), at] = part.astype(BF16)
            lanes = pl.ds(n * HEAD, HEAD)
            if s == 0:
                rows[:, lanes] = part.T.astype(BF16)
            else:
                rows_other[:, lanes] = part.T.astype(BF16)

    def gn_group(g):
        for slot in (2 * g, 2 * g + 1):
            share_msgs[SLOT_ORDER.index(slot)].wait_recv()
            part = mm_nt(rows[...], wq[slot].reshape(CHIP_D, 2 * QW)).astype(BF16)
            gn[slot] = part.reshape(2, 128, CHIP_D)
        gn_step0(g)

    def z_rows(dz):
        return pl.ds(pl.multiple_of(lax.rem(z + dz + 8, 8) * 16, 16), 16)

    zm_msgs = {}
    directions = ((zp, 1), (zm, -1))

    def gn_step0(g):
        for n, (target, _) in enumerate(directions):
            zm_msgs[g, 0, n] = send(gn.at[2 * g + n, :, z_rows(4)], zr0.at[n, g], target)

    def gn_step(g, step):
        for n, (target, sign) in enumerate(directions):
            at = z_rows(sign * (4 - step))
            zm_msgs[g, step - 1, n].wait_recv()
            if step == 1:
                mine = gn[2 * g + n, :, at, :].astype(F32)
                gn[2 * g + n, :, at, :] = (mine + zr0[n, g].astype(F32)).astype(BF16)
            else:
                mine = gn[pl.ds(2 * g, 2), :, at, :].astype(F32)
                mine = mine + zr1[n, g, step - 2].astype(F32)
                gn[pl.ds(2 * g, 2), :, at, :] = mine.astype(BF16)
            zm_msgs[g, step, n] = send(
                gn.at[pl.ds(2 * g, 2), :, at], zr1.at[n, g, step - 1], target
            )

    def gn_sum(g, which):
        at = z_rows(0)
        pair = pl.ds(2 * g, 2)
        total = gn[pair, which, at, :].astype(F32)
        return total + zr1[0, g, 2, :, which].astype(F32) + zr1[1, g, 2, :, which].astype(F32)

    def gn_exchange(g):
        for n in range(2):
            zm_msgs[g, 3, n].wait_recv()
        ysend[g] = gn_sum(g, 1 - yh).astype(BF16)
        zm_msgs[g, "y"] = send(ysend.at[g], yrecv.at[g], yhp)

    def gn_finish(g):
        zm_msgs[g, "y"].wait_recv()
        total = gn_sum(g, yh) + yrecv[g].astype(F32)
        for n in range(2):
            gnf[:, chip_cols(2 * g + n)] = total[n]

    def q_units(slot):
        weight_unit(gq, rows_t, nrm, slot)

    def norm_backward():
        total = gnf[...]
        standardized = xhat[...]
        mean_g = jnp.mean(total, axis=-1, keepdims=True)
        mean_p = jnp.mean(total * standardized, axis=-1, keepdims=True)
        hid_out[...] = (inv[:, :1] * (total - mean_g - standardized * mean_p)).astype(BF16)

    def await_up():
        loads[4].wait()
        up_msg.wait_recv()

    settled = []

    def settle(keep):
        for message in messages[len(settled):len(messages) - keep]:
            message.wait_send()
            settled.append(message)

    rows_msgs = []

    def share_rows():
        rows_msgs.append(send(rows_other, rows.at[:, pl.ds(QW, QW)], sib))

    def await_rows():
        rows_msgs[0].wait_recv()

    g_o.stage1()
    g_o.stage2()
    await_up()
    project_o(0)
    forward(0)
    forward(1)
    g_o.stage3()
    o_units(6)
    o_units(2)
    s_o.send_ya(2)
    project_o(4)
    s_o.send_xb1(1)
    project_o(3)
    g_o.stage4()
    o_units(0)
    o_units(4)
    project_o(1)
    g_o.stage5()
    project_o(7)
    s_o.send_xb1(0)
    s_o.send_ya(0)
    o_units(1)
    o_units(7)
    project_o(5)
    project_o(2)
    o_units(5)
    s_o.send_ya(1)
    s_o.step_xb2(1)
    s_o.step_xa1()
    s_o.send_ya(3)
    project_o(6)
    backward(1)
    share_rows()
    backward(0)
    q_units(6)
    s_q.send_ya(2)
    s_q.send_xb1(1)
    await_rows()
    gn_group(1)
    q_units(5)
    gn_group(2)
    q_units(2)
    q_units(7)
    s_q.send_xb1(0)
    gn_step(1, 1)
    s_q.send_ya(1)
    gn_group(0)
    gn_step(2, 1)
    s_q.step_xa1()
    s_q.send_ya(3)
    s_q.step_xb2(1)
    gn_step(1, 2)
    s_o.send_own()
    o_units(3)
    gn_group(3)
    gn_step(0, 1)
    gn_step(2, 2)
    q_units(4)
    q_units(0)
    s_o.step_xa2()
    q_units(1)
    s_q.send_own()
    s_q.send_ya(0)
    gn_step(3, 1)
    q_units(3)
    gn_step(1, 3)
    gn_step(0, 2)
    s_o.step_xb2(0)
    s_o.step_yb()
    s_q.step_xa2()
    gn_step(3, 2)
    s_q.step_yb()
    gn_step(2, 3)
    s_q.step_xb2(0)
    gn_step(0, 3)
    gn_step(3, 3)
    s_o.finish_a(go_out)
    gn_exchange(2)
    gn_exchange(1)
    gn_exchange(0)
    s_q.finish_a(gq_out)
    gn_exchange(3)
    s_o.finish_b(go_out)
    settle(16)
    gn_finish(2)
    gn_finish(1)
    s_q.finish_b(gq_out)
    gn_finish(0)
    gn_finish(3)
    norm_backward()

    settle(0)


def scatter_buffers(width):
    a = SCATTER_A[width]
    b = width - a
    return [
        pltpu.VMEM((3, a, CHIP_D), BF16),
        pltpu.VMEM((2, a, ROWS), BF16),
        pltpu.VMEM((2, 2, b, ROWS), BF16),
        pltpu.VMEM((2, b, CHIP_D), BF16),
        pltpu.VMEM((width, ROWS), BF16),
        pltpu.VMEM((2, a, ROWS), BF16),
        pltpu.VMEM((2, 2, a, ROWS), BF16),
        pltpu.VMEM((2, b, ROWS), BF16),
        pltpu.VMEM((2, 2, b, ROWS), BF16),
        pltpu.VMEM((2, a, ROWS), F32),
    ]


def hand_over_kernel(*refs):
    sources, targets, sem = refs[:3], refs[3:6], refs[6]
    copies = [
        pltpu.make_async_copy(a, b, sem.at[n]) for n, (a, b) in enumerate(zip(sources, targets))
    ]
    for copy in copies:
        copy.start()
    for copy in copies:
        copy.wait()


def hand_over(*arrays):
    return pl.pallas_call(
        hand_over_kernel,
        out_shape=tuple(jax.ShapeDtypeStruct(a.shape, a.dtype) for a in arrays),
        in_specs=[pl.BlockSpec(memory_space=pltpu.VMEM)] * 3,
        out_specs=(pl.BlockSpec(memory_space=pl.ANY),) * 3,
        scratch_shapes=[pltpu.SemaphoreType.DMA((3,))],
    )(*(pltpu.with_memory_space_constraint(a, pltpu.VMEM) for a in arrays))


def per_device(sublayer_input, w_qkv, w_out, upstream_grad):
    scratch = [
        pltpu.VMEM((ROWS, 2, QW), BF16),
        pltpu.VMEM((ROWS, 2, HEAD), BF16),
        pltpu.VMEM((2, ROWS, QW), BF16),
        pltpu.VMEM((2, ROWS, HEAD), BF16),
        pltpu.VMEM((N_CHIPS, 2, ROWS, 2 * QW), BF16),
        pltpu.VMEM((N_CHIPS, 2, ROWS, HEAD), BF16),
        pltpu.VMEM((2, SEQ, D), BF16),
        pltpu.VMEM((2, SEQ, D), BF16),
        pltpu.VMEM((SEQ, D), BF16),
        pltpu.VMEM((16, D), BF16),
        pltpu.VMEM((2 * SEQ, QW), F32),
        pltpu.VMEM((2 * SEQ, HEAD), F32),
        pltpu.VMEM((2 * SEQ, QW), BF16),
        pltpu.VMEM((2, SEQ, SEQ), F32),
        pltpu.VMEM((QW, 2 * SEQ), BF16),
        pltpu.VMEM((SEQ, 2 * QW), BF16),
        pltpu.VMEM((SEQ, QW), BF16),
        pltpu.VMEM((HEAD, 2 * SEQ), BF16),
        pltpu.VMEM((N_CHIPS, QW, CHIP_D), BF16),
        pltpu.VMEM((N_CHIPS, HEAD, CHIP_D), BF16),
        *scatter_buffers(QW),
        *scatter_buffers(HEAD),
        pltpu.VMEM((N_CHIPS, 2, 128, CHIP_D), BF16),
        pltpu.VMEM((2, GROUPS, 2, 16, CHIP_D), BF16),
        pltpu.VMEM((2, GROUPS, 3, 2, 2, 16, CHIP_D), BF16),
        pltpu.VMEM((GROUPS, 2, 16, CHIP_D), BF16),
        pltpu.VMEM((GROUPS, 2, 16, CHIP_D), BF16),
        pltpu.VMEM((16, D), F32),
        pltpu.VMEM((16, D), F32),
        pltpu.VMEM((16, 128), F32),
        pltpu.SemaphoreType.DMA((5,)),
        pltpu.SemaphoreType.DMA((N_MESSAGES,)),
        pltpu.SemaphoreType.DMA((N_MESSAGES,)),
    ]
    any_spec = pl.BlockSpec(memory_space=pl.ANY)
    vmem_spec = pl.BlockSpec(memory_space=pltpu.VMEM)
    hid, gq, go = pl.pallas_call(
        kernel,
        out_shape=(
            pltpu.VMEM((16, D), BF16),
            pltpu.VMEM((ROWS, 2, QW), F32),
            pltpu.VMEM((ROWS, 2, HEAD), F32),
        ),
        in_specs=[any_spec] * 4,
        out_specs=(vmem_spec,) * 3,
        scratch_shapes=scratch,
        compiler_params=pltpu.CompilerParams(
            collective_id=0, has_side_effects=True, vmem_limit_bytes=61 * 2**20
        ),
        cost_estimate=pl.CostEstimate(
            flops=10_000_000_000, bytes_accessed=10_000_000, transcendentals=200_000
        ),
    )(sublayer_input, w_qkv, w_out, upstream_grad)
    return hand_over(hid, gq, go)


def solution(mesh):
    in_specs = (P("dp", None), P("dp", "tensor", None), P("dp", "tensor", None), P("dp", None))
    out_specs = (P(("dp", "tensor"), None), P("dp", "tensor", None), P("dp", "tensor", None))
    return jax.shard_map(
        per_device, mesh=mesh, in_specs=in_specs, out_specs=out_specs, check_vma=False
    )
```

```python
import math

import jax
import jax.numpy as jnp
from jax import lax
from jax.experimental import pallas as pl
from jax.experimental.pallas import tpu as pltpu
from jax.sharding import PartitionSpec as P

EPS = 1e-05
MESH = pl.DeviceIdType.MESH
BF16 = jnp.bfloat16
F32 = jnp.float32

D = 6144
ROWS = 384
SEQ = 256
HEAD = 128
CHIP_D = 2 * ROWS
QW = 3 * HEAD
N_CHIPS = 8
N_DP = 16
GROUPS = 8
N_MESSAGES = 200
SLOT_ORDER = (0, 3, 1, 4, 7, 5, 2, 6)

GATHER_A, GATHER_A0, GATHER_B0 = 160, 80, 112
SCATTER_A = {QW: 160, HEAD: 48}


def mm(a, b):
    return lax.dot_general(a, b, (((1,), (0,)), ((), ())), preferred_element_type=F32)


def mm_nt(a, b):
    return lax.dot_general(a, b, (((1,), (1,)), ((), ())), preferred_element_type=F32)


def standardize(rows):
    centered = rows - jnp.mean(rows, axis=-1, keepdims=True)
    inverse_deviation = lax.rsqrt(jnp.mean(centered * centered, axis=-1, keepdims=True) + EPS)
    return centered * inverse_deviation, inverse_deviation


def kernel(
    x_hbm, wq_raw_hbm, wo_raw_hbm, up_hbm,
    hid_out, gq_out, go_out,
    wq_raw, wo_raw, wq_own, wo_own, wq, wo, nrm, up, xbuf, xrow, acc_q, acc_o, qkv, probs, rows_t, rows, rows_other, ctx_t,
    gq, go,
    q_ya, q_xa1, q_xb1, q_xb2, q_own, q_last_ya, q_last_xa, q_last_yb, q_last_xb, q_sum_a,
    o_ya, o_xa1, o_xb1, o_xb2, o_own, o_last_ya, o_last_xa, o_last_yb, o_last_xb, o_sum_a,
    gn, zr0, zr1, ysend, yrecv, gnf, xhat, inv,
    local_sem, send_sem, recv_sem,
):
    dp = lax.axis_index("dp")
    tn = lax.axis_index("tensor")
    core = lax.rem(dp, 2)
    other = 1 - core
    x = lax.rem(lax.div(dp, 2), 4)
    y = lax.div(dp, 8)
    z = lax.rem(tn, 8)
    yh = lax.div(tn, 8)

    def dp_at(yy, xx, cc):
        return (yy * 4 + xx) * 2 + cc

    sib = (dp_at(y, x, other), tn)
    xp = (dp_at(y, lax.rem(x + 1, 4), core), tn)
    xm = (dp_at(y, lax.rem(x + 3, 4), core), tn)
    yp = (dp_at(1 - y, x, core), tn)
    zp = (dp, yh * 8 + lax.rem(z + 1, 8))
    zm = (dp, yh * 8 + lax.rem(z + 7, 8))
    yhp = (dp, (1 - yh) * 8 + z)
    xp_other = (dp_at(y, lax.rem(x + 1, 4), other), tn)
    xm_other = (dp_at(y, lax.rem(x + 3, 4), other), tn)
    yp_other = (dp_at(1 - y, x, other), tn)
    partners = (sib, xp, xm, yp, zp, zm, yhp, xp_other, xm_other, yp_other)

    messages = []

    def send(src, dst, target):
        k = len(messages)
        copy = pltpu.make_async_remote_copy(
            src_ref=src, dst_ref=dst, send_sem=send_sem.at[k], recv_sem=recv_sem.at[k],
            device_id=target, device_id_type=MESH,
        )
        copy.start()
        messages.append(copy)
        return copy

    def chip_cols(slot):
        dy, dx = slot // 4, slot % 4
        chip = lax.rem(y + dy, 2) * 4 + lax.rem(x + dx, 4)
        return pl.ds(pl.multiple_of(chip * CHIP_D, 128), CHIP_D)

    def add_rows(n_rows, dst, *srcs):
        def body(r, carry):
            at = pl.ds(pl.multiple_of(r * 16, 16), 16)
            total = dst(at)[...].astype(F32)
            for src in srcs:
                total = total + src(at)[...].astype(F32)
            dst(at)[...] = total.astype(BF16)
            return carry

        lax.fori_loop(0, n_rows // 16, body, 0)

    barrier = pltpu.get_barrier_semaphore()
    for partner in partners:
        pl.semaphore_signal(barrier, inc=1, device_id=partner, device_id_type=MESH)
    token0 = pl.multiple_of(tn * 16, 16)
    loads = [
        pltpu.make_async_copy(x_hbm, xbuf, local_sem.at[0]),
        pltpu.make_async_copy(x_hbm.at[pl.ds(token0, 16)], xrow, local_sem.at[1]),
        pltpu.make_async_copy(wq_raw_hbm, wq_raw, local_sem.at[2]),
        pltpu.make_async_copy(wo_raw_hbm, wo_raw, local_sem.at[3]),
        pltpu.make_async_copy(up_hbm, up.at[0], local_sem.at[4]),
    ]
    loads[2].start()
    loads[3].start()
    loads[2].wait()
    loads[0].start()
    loads[1].start()
    for h in range(2):
        wq_own[h] = wq_raw[:, h, :]
    loads[3].wait()
    for h in range(2):
        wo_own[h] = wo_raw[:, h, :]
    own_loads = [
        pltpu.make_async_copy(wq_own.at[core], wq.at[0, core, :, pl.ds(0, QW)], local_sem.at[2]),
        pltpu.make_async_copy(wo_own.at[core], wo.at[0, core], local_sem.at[3]),
    ]
    for load in own_loads:
        load.start()
    pl.semaphore_wait(barrier, len(partners))

    A = pl.ds(0, GATHER_A)
    A0 = pl.ds(0, GATHER_A0)
    A1 = pl.ds(GATHER_A0, GATHER_A - GATHER_A0)
    B = pl.ds(GATHER_A, ROWS - GATHER_A)
    B0 = pl.ds(GATHER_A, GATHER_B0)
    B1 = pl.ds(GATHER_A + GATHER_B0, ROWS - GATHER_A - GATHER_B0)

    class Gather:
        def __init__(self, w, own, load, width):
            self.w, self.own, self.load, self.lanes = w, own, load, pl.ds(0, width)

        def at(self, slot, rows, part=slice(None)):
            return self.w.at[slot, part, rows, self.lanes]

        def move(self, slot, rows, to_slot, target):
            return send(self.at(slot, rows), self.at(to_slot, rows), target)

        def stage0(self):
            src = self.own
            self.swap = send(src.at[other], self.at(0, slice(None), core), sib)
            self.xa_p = [send(src.at[core, A], self.at(3, A, core), xp)]
            self.xa_m = [send(src.at[core, A], self.at(1, A, core), xm)]
            self.yb = [send(src.at[core, B], self.at(4, B, core), yp)]

        def stage0b(self):
            self.swap.wait_recv()
            self.xa_p.append(send(self.at(0, A, other), self.at(3, A, other), xp))
            self.xa_m.append(send(self.at(0, A, other), self.at(1, A, other), xm))
            self.yb.append(send(self.at(0, B, other), self.at(4, B, other), yp))
            self.load.wait()
            self.xb_p = self.move(0, B, 3, xp)
            self.xb_m = self.move(0, B, 1, xm)
            self.ya0 = self.move(0, A, 4, yp)

        def stage1(self):
            for m in self.xa_p:
                m.wait_recv()
            self.xa2_p = self.move(3, A0, 2, xp)
            for m in self.xa_m:
                m.wait_recv()
            self.xa2_m = self.move(1, A1, 2, xm)
            self.ya3 = self.move(3, A, 7, yp)
            self.ya1 = self.move(1, A, 5, yp)

        def stage2(self):
            for m in self.yb:
                m.wait_recv()
            self.xb3_p = self.move(4, B, 7, xp)
            self.xb3_m = self.move(4, B, 5, xm)

        def stage3(self):
            self.xb_p.wait_recv()
            self.xb2_p = self.move(3, B0, 2, xp)
            self.xb_m.wait_recv()
            self.xb2_m = self.move(1, B1, 2, xm)

        def stage4(self):
            self.xa2_p.wait_recv()
            self.ya2_p = self.move(2, A0, 6, yp)
            self.xa2_m.wait_recv()
            self.ya2_m = self.move(2, A1, 6, yp)

        def stage5(self):
            self.xb3_p.wait_recv()
            self.xb4_p = self.move(7, B0, 6, xp)
            self.xb3_m.wait_recv()
            self.xb4_m = self.move(5, B1, 6, xm)

        def complete(self, slot):
            pending = {
                0: (), 3: (), 1: (), 4: (self.ya0,),
                2: (self.xb2_p, self.xb2_m) if slot == 2 else (),
                7: (self.ya3,), 5: (self.ya1,),
                6: (self.ya2_p, self.ya2_m, self.xb4_p, self.xb4_m) if slot == 6 else (),
            }[slot]
            for m in pending:
                m.wait_recv()

    g_q = Gather(wq, wq_own, own_loads[0], QW)
    g_o = Gather(wo, wo_own, own_loads[1], HEAD)
    g_q.stage0()
    g_q.stage0b()

    loads[0].wait()

    def norm_rows(r, carry):
        at = pl.ds(pl.multiple_of(r * 16, 16), 16)
        standardized, _ = standardize(xbuf[at, :].astype(F32))
        nrm[0, at, :] = standardized.astype(BF16)
        return carry

    lax.fori_loop(0, SEQ // 16, norm_rows, 0)
    nrm_msg = send(nrm.at[0], nrm.at[1], sib)

    def project(acc, w, left, width, slot):
        a = left[:, :, chip_cols(slot)].reshape(2 * SEQ, CHIP_D)
        product = mm(a, w[slot, :, :, pl.ds(0, width)].reshape(CHIP_D, width))
        if slot == 0:
            acc[...] = product
        else:
            acc[...] += product

    share_msgs = []

    def project_q(slot):
        g_q.complete(slot)
        share_msgs.append(send(
            wq.at[slot, :, :, pl.ds(0, QW)], wq.at[slot, :, :, pl.ds(QW, QW)], sib
        ))
        project(acc_q, wq, nrm, QW, slot)

    def project_o(slot):
        g_o.complete(slot)
        project(acc_o, wo, up, HEAD, slot)

    g_q.stage1()
    g_q.stage2()
    loads[4].start()
    up_msg = send(up_hbm, up.at[1], sib)
    loads[1].wait()
    own_xhat, own_inv = standardize(xrow[...].astype(F32))
    xhat[...] = own_xhat
    inv[...] = jnp.broadcast_to(own_inv, (16, 128))
    nrm_msg.wait_recv()
    project_q(0)
    g_q.stage3()
    project_q(3)
    g_q.stage4()
    project_q(1)
    project_q(4)
    g_q.stage5()
    g_o.stage0()
    project_q(7)
    g_o.stage0b()
    project_q(5)
    project_q(2)
    project_q(6)
    qkv[...] = acc_q[...].astype(BF16)

    scale = 1.0 / math.sqrt(HEAD)

    def forward(s):
        at = pl.ds(s * SEQ, SEQ)
        query, key, value = (qkv[at, pl.ds(n * HEAD, HEAD)] for n in range(3))
        raised = jnp.exp(mm_nt(query, key) * scale)
        attn = raised / jnp.sum(raised, axis=-1, keepdims=True)
        probs[s] = attn
        context = mm(attn.astype(BF16), value).astype(BF16).astype(F32)
        ctx_t[:, at] = context.T.astype(BF16)

    def weight_unit(g, left_t, right, slot):
        b = right[:, :, chip_cols(slot)].reshape(2 * SEQ, CHIP_D)
        g[slot] = mm(left_t[...], b).astype(BF16)

    L = (pl.ds(0, ROWS), pl.ds(ROWS, ROWS))

    def lanes_of(cc):
        return pl.ds(pl.multiple_of(cc * ROWS, 128), ROWS)

    class Scatter:
        def __init__(
            self, g, width, ya, xa1, xb1, xb2, own, last_ya, last_xa, last_yb, last_xb, sum_a
        ):
            self.g, self.width = g, width
            self.na = SCATTER_A[width]
            self.nb = width - self.na
            self.A, self.B = pl.ds(0, self.na), pl.ds(self.na, self.nb)
            self.ya, self.xa1, self.xb1, self.xb2, self.own = ya, xa1, xb1, xb2, own
            self.last_ya, self.last_xa, self.last_yb, self.last_xb = last_ya, last_xa, last_yb, last_xb
            self.sum_a = sum_a
            self.m = {}

        def rows_a(self, slot, lanes=slice(None)):
            return lambda at: self.g.at[slot, at, lanes]

        def rows_b(self, slot, lanes=slice(None)):
            def view(at):
                return self.g.at[slot, pl.ds(pl.multiple_of(at.start + self.na, 16), 16), lanes]

            return view

        def last_hop(self, slot, rows, buf, target, target_other):
            return [
                send(self.g.at[slot, rows, lanes_of(cc)], buf.at[core], to)
                for cc, to in ((core, target), (other, target_other))
            ]

        def send_own(self):
            self.m["own"] = [send(self.g.at[0, :, lanes_of(other)], self.own, sib)]

        def send_ya(self, dx):
            if dx == 0:
                self.m["ya", 0] = self.last_hop(4, self.A, self.last_ya, yp, yp_other)
            else:
                self.m["ya", dx] = send(self.g.at[4 + dx, self.A], self.ya.at[dx - 1], yp)

        def send_xb1(self, dy):
            for n, target in enumerate((xp, xm)):
                self.m["xb1", dy, n] = send(
                    self.g.at[dy * 4 + 2, self.B, L[n]], self.xb1.at[dy, n], target
                )

        def step_xb2(self, dy):
            for n, (slot, target, target_other) in enumerate(((1, xp, xp_other), (3, xm, xm_other))):
                self.m["xb1", dy, n].wait_recv()
                at_slot = dy * 4 + slot
                add_rows(
                    self.nb, self.rows_b(at_slot, L[n]), lambda at, n=n: self.xb1.at[dy, n, at]
                )
                if dy == 0:
                    self.m["xb2", 0, n] = self.last_hop(
                        at_slot, self.B, self.last_xb.at[n], target, target_other
                    )
                else:
                    self.m["xb2", 1, n] = send(self.g.at[at_slot, self.B], self.xb2.at[n], target)

        def step_xa1(self):
            self.m["ya", 2].wait_recv()
            add_rows(self.na, self.rows_a(2), lambda at: self.ya.at[1, at])
            for n, target in enumerate((xp, xm)):
                self.m["xa1", n] = send(self.g.at[2, self.A, L[n]], self.xa1.at[n], target)

        def step_xa2(self):
            for n, (slot, target, target_other) in enumerate(((1, xp, xp_other), (3, xm, xm_other))):
                self.m["ya", slot].wait_recv()
                self.m["xa1", n].wait_recv()
                add_rows(
                    self.na, self.rows_a(slot, L[n]),
                    lambda at, n=n, slot=slot: self.ya.at[slot - 1, at, L[n]],
                    lambda at, n=n: self.xa1.at[n, at],
                )
                add_rows(
                    self.na, self.rows_a(slot, L[1 - n]),
                    lambda at, n=n, slot=slot: self.ya.at[slot - 1, at, L[1 - n]],
                )
                self.m["xa2", n] = self.last_hop(
                    slot, self.A, self.last_xa.at[n], target, target_other
                )

        def step_yb(self):
            for n in range(2):
                self.m["xb2", 1, n].wait_recv()
            add_rows(
                self.nb, self.rows_b(4),
                lambda at: self.xb2.at[0, at], lambda at: self.xb2.at[1, at],
            )
            self.m["yb"] = self.last_hop(4, self.B, self.last_yb, yp, yp_other)

        def total(self, rows, h, *received):
            mine = self.g[0, rows, lanes_of(core)].astype(F32)
            total = jnp.where(core == h, mine, self.own[rows, :].astype(F32))
            for part in received:
                total = total + part.astype(F32)
            return total * (1.0 / N_DP)

        def wait_last(self, *keys):
            for key in keys:
                for message in self.m[key]:
                    message.wait_recv()

        def write(self, out, value, fb, h):
            out[:, h, pl.ds(fb * HEAD, HEAD)] = value.T

        def finish_a(self, out):
            self.wait_last("own", ("ya", 0), ("xa2", 0), ("xa2", 1))
            for h in range(2):
                total = self.total(
                    self.A, h, self.last_ya[h], self.last_xa[0, h], self.last_xa[1, h]
                )
                self.sum_a[h] = total
                if self.na >= HEAD:
                    self.write(out, total[:HEAD], 0, h)

        def finish_b(self, out):
            self.wait_last(("xb2", 0, 0), ("xb2", 0, 1), "yb")
            done = self.na // HEAD
            for h in range(2):
                total = self.total(
                    self.B, h, self.last_yb[h], self.last_xb[0, h], self.last_xb[1, h]
                )
                rest = jnp.concatenate([self.sum_a[h, done * HEAD:, :], total], axis=0)
                for fb in range(done, self.width // HEAD):
                    at = (fb - done) * HEAD
                    self.write(out, rest[at:at + HEAD], fb, h)

    s_o = Scatter(
        go, HEAD, o_ya, o_xa1, o_xb1, o_xb2, o_own,
        o_last_ya, o_last_xa, o_last_yb, o_last_xb, o_sum_a,
    )
    s_q = Scatter(
        gq, QW, q_ya, q_xa1, q_xb1, q_xb2, q_own,
        q_last_ya, q_last_xa, q_last_yb, q_last_xb, q_sum_a,
    )

    def o_units(slot):
        weight_unit(go, ctx_t, up, slot)

    def backward(s):
        at = pl.ds(s * SEQ, SEQ)
        query, key, value = (qkv[at, pl.ds(n * HEAD, HEAD)] for n in range(3))
        grad_context = acc_o[at, :].astype(BF16)
        attn = probs[s]
        grad_prob = mm_nt(grad_context, value)
        row_dot = jnp.sum(attn * grad_prob, axis=-1, keepdims=True)
        grad_score = (attn * (grad_prob - row_dot) * scale).astype(BF16)
        query_t = query.astype(F32).T.astype(BF16)
        key_t = key.astype(F32).T.astype(BF16)
        grad_context_t = grad_context.astype(F32).T.astype(BF16)
        parts = (
            mm_nt(key_t, grad_score),
            mm(query_t, grad_score),
            mm(grad_context_t, attn.astype(BF16)),
        )
        for n, part in enumerate(parts):
            rows_t[pl.ds(n * HEAD, HEAD), at] = part.astype(BF16)
            lanes = pl.ds(n * HEAD, HEAD)
            if s == 0:
                rows[:, lanes] = part.T.astype(BF16)
            else:
                rows_other[:, lanes] = part.T.astype(BF16)

    def gn_group(g):
        share_msgs[SLOT_ORDER.index(g)].wait_recv()
        part = mm_nt(rows[...], wq[g].reshape(CHIP_D, 2 * QW)).astype(BF16)
        gn[g] = part.reshape(2, 128, CHIP_D)
        gn_step0(g)

    def z_rows(dz):
        return pl.ds(pl.multiple_of(lax.rem(z + dz + 8, 8) * 16, 16), 16)

    zm_msgs = {}
    directions = ((zp, 1), (zm, -1))

    def gn_step0(g):
        for n, (target, _) in enumerate(directions):
            zm_msgs[g, 0, n] = send(gn.at[g, n, z_rows(4)], zr0.at[n, g], target)

    def gn_step(g, step):
        for n, (target, sign) in enumerate(directions):
            at = z_rows(sign * (4 - step))
            zm_msgs[g, step - 1, n].wait_recv()
            if step == 1:
                mine = gn[g, n, at, :].astype(F32)
                gn[g, n, at, :] = (mine + zr0[n, g].astype(F32)).astype(BF16)
            else:
                mine = gn[g, :, at, :].astype(F32)
                gn[g, :, at, :] = (mine + zr1[n, g, step - 2].astype(F32)).astype(BF16)
            zm_msgs[g, step, n] = send(gn.at[g, :, at], zr1.at[n, g, step - 1], target)

    def gn_sum(g, which):
        total = gn[g, which, z_rows(0), :].astype(F32)
        return total + zr1[0, g, 2, which].astype(F32) + zr1[1, g, 2, which].astype(F32)

    def gn_exchange(g):
        for n in range(2):
            zm_msgs[g, 3, n].wait_recv()
        ysend[g] = gn_sum(g, 1 - yh).astype(BF16)
        zm_msgs[g, "y"] = send(ysend.at[g], yrecv.at[g], yhp)

    def gn_finish(g):
        zm_msgs[g, "y"].wait_recv()
        gnf[:, chip_cols(g)] = gn_sum(g, yh) + yrecv[g].astype(F32)

    def q_units(slot):
        weight_unit(gq, rows_t, nrm, slot)

    def norm_backward():
        total = gnf[...]
        standardized = xhat[...]
        mean_g = jnp.mean(total, axis=-1, keepdims=True)
        mean_p = jnp.mean(total * standardized, axis=-1, keepdims=True)
        hid_out[...] = (inv[:, :1] * (total - mean_g - standardized * mean_p)).astype(BF16)

    def await_up():
        loads[4].wait()
        up_msg.wait_recv()

    settled = []

    def settle(keep):
        for message in messages[len(settled):len(messages) - keep]:
            message.wait_send()
            settled.append(message)

    rows_msgs = []

    def share_rows():
        rows_msgs.append(send(rows_other, rows.at[:, pl.ds(QW, QW)], sib))

    def await_rows():
        rows_msgs[0].wait_recv()

    g_o.stage1()
    g_o.stage2()
    forward(0)
    await_up()
    forward(1)
    o_units(6)
    project_o(0)
    g_o.stage3()
    project_o(4)
    o_units(1)
    s_o.send_xb1(1)
    s_o.send_ya(2)
    o_units(4)
    o_units(5)
    o_units(7)
    o_units(3)
    g_o.stage4()
    o_units(2)
    g_o.stage5()
    project_o(3)
    s_o.send_ya(3)
    s_o.send_ya(1)
    project_o(1)
    s_o.send_ya(0)
    s_o.send_xb1(0)
    project_o(7)
    project_o(5)
    s_o.step_xa1()
    s_o.step_xb2(1)
    project_o(2)
    project_o(6)
    backward(1)
    share_rows()
    backward(0)
    q_units(6)
    s_q.send_ya(2)
    await_rows()
    s_q.send_xb1(1)
    gn_group(6)
    gn_group(5)
    gn_group(7)
    gn_group(2)
    q_units(2)
    s_q.send_xb1(0)
    q_units(7)
    gn_step(6, 1)
    gn_group(0)
    gn_step(5, 1)
    s_q.send_ya(3)
    gn_group(3)
    gn_step(7, 1)
    gn_step(2, 1)
    s_o.step_xb2(0)
    gn_group(4)
    gn_step(6, 2)
    s_q.step_xa1()
    q_units(5)
    s_q.send_ya(1)
    gn_step(5, 2)
    gn_group(1)
    gn_step(0, 1)
    s_q.step_xb2(1)
    gn_step(4, 1)
    gn_step(3, 1)
    gn_step(7, 2)
    q_units(4)
    q_units(3)
    s_q.send_ya(0)
    s_o.step_yb()
    gn_step(5, 3)
    gn_step(1, 1)
    gn_step(2, 2)
    gn_step(0, 2)
    q_units(1)
    gn_step(4, 2)
    s_o.step_xa2()
    gn_step(3, 2)
    s_q.step_xa2()
    gn_step(6, 3)
    gn_step(1, 2)
    gn_exchange(5)
    s_q.step_yb()
    gn_step(7, 3)
    gn_step(0, 3)
    gn_step(4, 3)
    s_q.step_xb2(0)
    o_units(0)
    gn_step(2, 3)
    gn_step(3, 3)
    q_units(0)
    s_o.send_own()
    gn_exchange(7)
    gn_step(1, 3)
    s_o.finish_a(go_out)
    gn_exchange(4)
    gn_exchange(6)
    gn_finish(5)
    s_q.send_own()
    gn_exchange(0)
    s_o.finish_b(go_out)
    gn_exchange(3)
    gn_exchange(2)
    gn_exchange(1)
    s_q.finish_a(gq_out)
    gn_finish(7)
    gn_finish(4)
    settle(24)
    gn_finish(6)
    s_q.finish_b(gq_out)
    gn_finish(3)
    gn_finish(0)
    gn_finish(2)
    gn_finish(1)
    norm_backward()

    settle(0)


def scatter_buffers(width):
    a = SCATTER_A[width]
    b = width - a
    return [
        pltpu.VMEM((3, a, CHIP_D), BF16),
        pltpu.VMEM((2, a, ROWS), BF16),
        pltpu.VMEM((2, 2, b, ROWS), BF16),
        pltpu.VMEM((2, b, CHIP_D), BF16),
        pltpu.VMEM((width, ROWS), BF16),
        pltpu.VMEM((2, a, ROWS), BF16),
        pltpu.VMEM((2, 2, a, ROWS), BF16),
        pltpu.VMEM((2, b, ROWS), BF16),
        pltpu.VMEM((2, 2, b, ROWS), BF16),
        pltpu.VMEM((2, a, ROWS), F32),
    ]


def hand_over_kernel(*refs):
    sources, targets, sem = refs[:3], refs[3:6], refs[6]
    copies = [
        pltpu.make_async_copy(a, b, sem.at[n]) for n, (a, b) in enumerate(zip(sources, targets))
    ]
    for copy in copies:
        copy.start()
    for copy in copies:
        copy.wait()


def hand_over(*arrays):
    return pl.pallas_call(
        hand_over_kernel,
        out_shape=tuple(jax.ShapeDtypeStruct(a.shape, a.dtype) for a in arrays),
        in_specs=[pl.BlockSpec(memory_space=pltpu.VMEM)] * 3,
        out_specs=(pl.BlockSpec(memory_space=pl.ANY),) * 3,
        scratch_shapes=[pltpu.SemaphoreType.DMA((3,))],
    )(*(pltpu.with_memory_space_constraint(a, pltpu.VMEM) for a in arrays))


def per_device(sublayer_input, w_qkv, w_out, upstream_grad):
    scratch = [
        pltpu.VMEM((ROWS, 2, QW), BF16),
        pltpu.VMEM((ROWS, 2, HEAD), BF16),
        pltpu.VMEM((2, ROWS, QW), BF16),
        pltpu.VMEM((2, ROWS, HEAD), BF16),
        pltpu.VMEM((N_CHIPS, 2, ROWS, 2 * QW), BF16),
        pltpu.VMEM((N_CHIPS, 2, ROWS, HEAD), BF16),
        pltpu.VMEM((2, SEQ, D), BF16),
        pltpu.VMEM((2, SEQ, D), BF16),
        pltpu.VMEM((SEQ, D), BF16),
        pltpu.VMEM((16, D), BF16),
        pltpu.VMEM((2 * SEQ, QW), F32),
        pltpu.VMEM((2 * SEQ, HEAD), F32),
        pltpu.VMEM((2 * SEQ, QW), BF16),
        pltpu.VMEM((2, SEQ, SEQ), F32),
        pltpu.VMEM((QW, 2 * SEQ), BF16),
        pltpu.VMEM((SEQ, 2 * QW), BF16),
        pltpu.VMEM((SEQ, QW), BF16),
        pltpu.VMEM((HEAD, 2 * SEQ), BF16),
        pltpu.VMEM((N_CHIPS, QW, CHIP_D), BF16),
        pltpu.VMEM((N_CHIPS, HEAD, CHIP_D), BF16),
        *scatter_buffers(QW),
        *scatter_buffers(HEAD),
        pltpu.VMEM((N_CHIPS, 2, 128, CHIP_D), BF16),
        pltpu.VMEM((2, GROUPS, 16, CHIP_D), BF16),
        pltpu.VMEM((2, GROUPS, 3, 2, 16, CHIP_D), BF16),
        pltpu.VMEM((GROUPS, 16, CHIP_D), BF16),
        pltpu.VMEM((GROUPS, 16, CHIP_D), BF16),
        pltpu.VMEM((16, D), F32),
        pltpu.VMEM((16, D), F32),
        pltpu.VMEM((16, 128), F32),
        pltpu.SemaphoreType.DMA((5,)),
        pltpu.SemaphoreType.DMA((N_MESSAGES,)),
        pltpu.SemaphoreType.DMA((N_MESSAGES,)),
    ]
    any_spec = pl.BlockSpec(memory_space=pl.ANY)
    vmem_spec = pl.BlockSpec(memory_space=pltpu.VMEM)
    hid, gq, go = pl.pallas_call(
        kernel,
        out_shape=(
            pltpu.VMEM((16, D), BF16),
            pltpu.VMEM((ROWS, 2, QW), F32),
            pltpu.VMEM((ROWS, 2, HEAD), F32),
        ),
        in_specs=[any_spec] * 4,
        out_specs=(vmem_spec,) * 3,
        scratch_shapes=scratch,
        compiler_params=pltpu.CompilerParams(
            collective_id=0, has_side_effects=True, vmem_limit_bytes=61 * 2**20
        ),
        cost_estimate=pl.CostEstimate(
            flops=10_000_000_000, bytes_accessed=10_000_000, transcendentals=200_000
        ),
    )(sublayer_input, w_qkv, w_out, upstream_grad)
    return hand_over(hid, gq, go)


def solution(mesh):
    in_specs = (P("dp", None), P("dp", "tensor", None), P("dp", "tensor", None), P("dp", None))
    out_specs = (P(("dp", "tensor"), None), P("dp", "tensor", None), P("dp", "tensor", None))
    return jax.shard_map(
        per_device, mesh=mesh, in_specs=in_specs, out_specs=out_specs, check_vma=False
    )
```

```python
import math

import jax
import jax.numpy as jnp
from jax import lax
from jax.experimental import pallas as pl
from jax.experimental.pallas import tpu as pltpu
from jax.sharding import PartitionSpec as P

EPS = 1e-05
MESH = pl.DeviceIdType.MESH
BF16 = jnp.bfloat16
F32 = jnp.float32

D = 6144
ROWS = 384
SEQ = 256
HEAD = 128
CHIP_D = 2 * ROWS
QW = 3 * HEAD
N_CHIPS = 8
N_DP = 16
GROUPS = 8
N_MESSAGES = 200
SLOT_ORDER = (0, 3, 1, 4, 7, 5, 2, 6)

GATHER_A, GATHER_A0, GATHER_B0 = 160, 80, 112
SCATTER_A = {QW: 160, HEAD: 48}


def mm(a, b):
    return lax.dot_general(a, b, (((1,), (0,)), ((), ())), preferred_element_type=F32)


def mm_nt(a, b):
    return lax.dot_general(a, b, (((1,), (1,)), ((), ())), preferred_element_type=F32)


def standardize(rows):
    centered = rows - jnp.mean(rows, axis=-1, keepdims=True)
    inverse_deviation = lax.rsqrt(jnp.mean(centered * centered, axis=-1, keepdims=True) + EPS)
    return centered * inverse_deviation, inverse_deviation


def kernel(
    x_hbm, wq_raw_hbm, wo_raw_hbm, up_hbm,
    hid_out, gq_out, go_out,
    wq_raw, wo_raw, wq_own, wo_own, wq, wo, nrm, up, xbuf, xrow, acc_q, acc_o, qkv, probs, rows_t, rows, rows_other, ctx_t,
    gq, go,
    q_ya, q_xa1, q_xb1, q_xb2, q_own, q_last_ya, q_last_xa, q_last_yb, q_last_xb, q_sum_a,
    o_ya, o_xa1, o_xb1, o_xb2, o_own, o_last_ya, o_last_xa, o_last_yb, o_last_xb, o_sum_a,
    gn, zr0, zr1, ysend, yrecv, gnf, xhat, inv,
    local_sem, send_sem, recv_sem,
):
    dp = lax.axis_index("dp")
    tn = lax.axis_index("tensor")
    core = lax.rem(dp, 2)
    other = 1 - core
    x = lax.rem(lax.div(dp, 2), 4)
    y = lax.div(dp, 8)
    z = lax.rem(tn, 8)
    yh = lax.div(tn, 8)

    def dp_at(yy, xx, cc):
        return (yy * 4 + xx) * 2 + cc

    sib = (dp_at(y, x, other), tn)
    xp = (dp_at(y, lax.rem(x + 1, 4), core), tn)
    xm = (dp_at(y, lax.rem(x + 3, 4), core), tn)
    yp = (dp_at(1 - y, x, core), tn)
    zp = (dp, yh * 8 + lax.rem(z + 1, 8))
    zm = (dp, yh * 8 + lax.rem(z + 7, 8))
    yhp = (dp, (1 - yh) * 8 + z)
    xp_other = (dp_at(y, lax.rem(x + 1, 4), other), tn)
    xm_other = (dp_at(y, lax.rem(x + 3, 4), other), tn)
    yp_other = (dp_at(1 - y, x, other), tn)
    partners = (sib, xp, xm, yp, zp, zm, yhp, xp_other, xm_other, yp_other)

    messages = []

    def send(src, dst, target):
        k = len(messages)
        copy = pltpu.make_async_remote_copy(
            src_ref=src, dst_ref=dst, send_sem=send_sem.at[k], recv_sem=recv_sem.at[k],
            device_id=target, device_id_type=MESH,
        )
        copy.start()
        messages.append(copy)
        return copy

    def chip_cols(slot):
        dy, dx = slot // 4, slot % 4
        chip = lax.rem(y + dy, 2) * 4 + lax.rem(x + dx, 4)
        return pl.ds(pl.multiple_of(chip * CHIP_D, 128), CHIP_D)

    def add_rows(n_rows, dst, *srcs):
        def body(r, carry):
            at = pl.ds(pl.multiple_of(r * 16, 16), 16)
            total = dst(at)[...].astype(F32)
            for src in srcs:
                total = total + src(at)[...].astype(F32)
            dst(at)[...] = total.astype(BF16)
            return carry

        lax.fori_loop(0, n_rows // 16, body, 0)

    barrier = pltpu.get_barrier_semaphore()
    for partner in partners:
        pl.semaphore_signal(barrier, inc=1, device_id=partner, device_id_type=MESH)
    token0 = pl.multiple_of(tn * 16, 16)
    loads = [
        pltpu.make_async_copy(x_hbm, xbuf, local_sem.at[0]),
        pltpu.make_async_copy(x_hbm.at[pl.ds(token0, 16)], xrow, local_sem.at[1]),
        pltpu.make_async_copy(wq_raw_hbm, wq_raw, local_sem.at[2]),
        pltpu.make_async_copy(wo_raw_hbm, wo_raw, local_sem.at[3]),
        pltpu.make_async_copy(up_hbm, up.at[0], local_sem.at[4]),
    ]
    loads[2].start()
    loads[3].start()
    loads[2].wait()
    loads[0].start()
    loads[1].start()
    for h in range(2):
        wq_own[h, :GATHER_A] = wq_raw[:GATHER_A, h, :]
    own_loads = [
        pltpu.make_async_copy(wq_own.at[core], wq.at[0, core, :, pl.ds(0, QW)], local_sem.at[2]),
        pltpu.make_async_copy(wo_own.at[core], wo.at[0, core], local_sem.at[3]),
    ]
    pl.semaphore_wait(barrier, len(partners))

    A = pl.ds(0, GATHER_A)
    A0 = pl.ds(0, GATHER_A0)
    A1 = pl.ds(GATHER_A0, GATHER_A - GATHER_A0)
    B = pl.ds(GATHER_A, ROWS - GATHER_A)
    B0 = pl.ds(GATHER_A, GATHER_B0)
    B1 = pl.ds(GATHER_A + GATHER_B0, ROWS - GATHER_A - GATHER_B0)

    class Gather:
        def __init__(self, w, own, load, width, split):
            self.w, self.own, self.load, self.lanes = w, own, load, pl.ds(0, width)
            self.split = split

        def at(self, slot, rows, part=slice(None)):
            return self.w.at[slot, part, rows, self.lanes]

        def move(self, slot, rows, to_slot, target):
            return send(self.at(slot, rows), self.at(to_slot, rows), target)

        def stage0(self):
            src = self.own
            self.xa_p = [send(src.at[core, A], self.at(3, A, core), xp)]
            self.xa_m = [send(src.at[core, A], self.at(1, A, core), xm)]
            self.split()
            self.yb = [send(src.at[core, B], self.at(4, B, core), yp)]
            self.swap = send(src.at[other], self.at(0, slice(None), core), sib)
            self.load.start()

        def stage0b(self):
            self.swap.wait_recv()
            self.xa_p.append(send(self.at(0, A, other), self.at(3, A, other), xp))
            self.xa_m.append(send(self.at(0, A, other), self.at(1, A, other), xm))
            self.yb.append(send(self.at(0, B, other), self.at(4, B, other), yp))
            self.load.wait()
            self.xb_p = self.move(0, B, 3, xp)
            self.xb_m = self.move(0, B, 1, xm)
            self.ya0 = self.move(0, A, 4, yp)

        def stage1(self):
            for m in self.xa_p:
                m.wait_recv()
            self.xa2_p = self.move(3, A0, 2, xp)
            for m in self.xa_m:
                m.wait_recv()
            self.xa2_m = self.move(1, A1, 2, xm)
            self.ya3 = self.move(3, A, 7, yp)
            self.ya1 = self.move(1, A, 5, yp)

        def stage2(self):
            for m in self.yb:
                m.wait_recv()
            self.xb3_p = self.move(4, B, 7, xp)
            self.xb3_m = self.move(4, B, 5, xm)

        def stage3(self):
            self.xb_p.wait_recv()
            self.xb2_p = self.move(3, B0, 2, xp)
            self.xb_m.wait_recv()
            self.xb2_m = self.move(1, B1, 2, xm)

        def stage4(self):
            self.xa2_p.wait_recv()
            self.ya2_p = self.move(2, A0, 6, yp)
            self.xa2_m.wait_recv()
            self.ya2_m = self.move(2, A1, 6, yp)

        def stage5(self):
            self.xb3_p.wait_recv()
            self.xb4_p = self.move(7, B0, 6, xp)
            self.xb3_m.wait_recv()
            self.xb4_m = self.move(5, B1, 6, xm)

        def complete(self, slot):
            pending = {
                0: (), 3: (), 1: (), 4: (self.ya0,),
                2: (self.xb2_p, self.xb2_m) if slot == 2 else (),
                7: (self.ya3,), 5: (self.ya1,),
                6: (self.ya2_p, self.ya2_m, self.xb4_p, self.xb4_m) if slot == 6 else (),
            }[slot]
            for m in pending:
                m.wait_recv()

    def split_q():
        for h in range(2):
            wq_own[h, GATHER_A:] = wq_raw[GATHER_A:, h, :]

    def split_o():
        loads[3].wait()
        for h in range(2):
            wo_own[h] = wo_raw[:, h, :]

    g_q = Gather(wq, wq_own, own_loads[0], QW, split_q)
    g_o = Gather(wo, wo_own, own_loads[1], HEAD, lambda: None)
    g_q.stage0()
    split_o()
    g_q.stage0b()

    loads[0].wait()

    def norm_rows(r, carry):
        at = pl.ds(pl.multiple_of(r * 16, 16), 16)
        standardized, _ = standardize(xbuf[at, :].astype(F32))
        nrm[0, at, :] = standardized.astype(BF16)
        return carry

    lax.fori_loop(0, SEQ // 16, norm_rows, 0)
    nrm_msg = send(nrm.at[0], nrm.at[1], sib)

    def project(acc, w, left, width, slot):
        a = left[:, :, chip_cols(slot)].reshape(2 * SEQ, CHIP_D)
        product = mm(a, w[slot, :, :, pl.ds(0, width)].reshape(CHIP_D, width))
        if slot == 0:
            acc[...] = product
        else:
            acc[...] += product

    share_msgs = []

    def project_q(slot):
        g_q.complete(slot)
        share_msgs.append(send(
            wq.at[slot, :, :, pl.ds(0, QW)], wq.at[slot, :, :, pl.ds(QW, QW)], sib
        ))
        project(acc_q, wq, nrm, QW, slot)

    def project_o(slot):
        g_o.complete(slot)
        project(acc_o, wo, up, HEAD, slot)

    g_q.stage1()
    g_q.stage2()
    loads[4].start()
    up_msg = send(up_hbm, up.at[1], sib)
    loads[1].wait()
    own_xhat, own_inv = standardize(xrow[...].astype(F32))
    xhat[...] = own_xhat
    inv[...] = jnp.broadcast_to(own_inv, (16, 128))
    nrm_msg.wait_recv()
    project_q(0)
    g_q.stage3()
    project_q(3)
    g_q.stage4()
    project_q(1)
    project_q(4)
    g_q.stage5()
    g_o.stage0()
    project_q(7)
    g_o.stage0b()
    project_q(5)
    project_q(2)
    project_q(6)
    qkv[...] = acc_q[...].astype(BF16)

    scale = 1.0 / math.sqrt(HEAD)

    def forward(s):
        at = pl.ds(s * SEQ, SEQ)
        query, key, value = (qkv[at, pl.ds(n * HEAD, HEAD)] for n in range(3))
        raised = jnp.exp(mm_nt(query, key) * scale)
        attn = raised / jnp.sum(raised, axis=-1, keepdims=True)
        probs[s] = attn
        context = mm(attn.astype(BF16), value).astype(BF16).astype(F32)
        ctx_t[:, at] = context.T.astype(BF16)

    def weight_unit(g, left_t, right, slot):
        b = right[:, :, chip_cols(slot)].reshape(2 * SEQ, CHIP_D)
        g[slot] = mm(left_t[...], b).astype(BF16)

    L = (pl.ds(0, ROWS), pl.ds(ROWS, ROWS))

    def lanes_of(cc):
        return pl.ds(pl.multiple_of(cc * ROWS, 128), ROWS)

    class Scatter:
        def __init__(
            self, g, width, ya, xa1, xb1, xb2, own, last_ya, last_xa, last_yb, last_xb, sum_a
        ):
            self.g, self.width = g, width
            self.na = SCATTER_A[width]
            self.nb = width - self.na
            self.A, self.B = pl.ds(0, self.na), pl.ds(self.na, self.nb)
            self.ya, self.xa1, self.xb1, self.xb2, self.own = ya, xa1, xb1, xb2, own
            self.last_ya, self.last_xa, self.last_yb, self.last_xb = last_ya, last_xa, last_yb, last_xb
            self.sum_a = sum_a
            self.m = {}

        def rows_a(self, slot, lanes=slice(None)):
            return lambda at: self.g.at[slot, at, lanes]

        def rows_b(self, slot, lanes=slice(None)):
            def view(at):
                return self.g.at[slot, pl.ds(pl.multiple_of(at.start + self.na, 16), 16), lanes]

            return view

        def last_hop(self, slot, rows, buf, target, target_other):
            return [
                send(self.g.at[slot, rows, lanes_of(cc)], buf.at[core], to)
                for cc, to in ((core, target), (other, target_other))
            ]

        def send_own(self):
            self.m["own"] = [send(self.g.at[0, :, lanes_of(other)], self.own, sib)]

        def send_ya(self, dx):
            if dx == 0:
                self.m["ya", 0] = self.last_hop(4, self.A, self.last_ya, yp, yp_other)
            else:
                self.m["ya", dx] = send(self.g.at[4 + dx, self.A], self.ya.at[dx - 1], yp)

        def send_xb1(self, dy):
            for n, target in enumerate((xp, xm)):
                self.m["xb1", dy, n] = send(
                    self.g.at[dy * 4 + 2, self.B, L[n]], self.xb1.at[dy, n], target
                )

        def step_xb2(self, dy):
            for n, (slot, target, target_other) in enumerate(((1, xp, xp_other), (3, xm, xm_other))):
                self.m["xb1", dy, n].wait_recv()
                at_slot = dy * 4 + slot
                add_rows(
                    self.nb, self.rows_b(at_slot, L[n]), lambda at, n=n: self.xb1.at[dy, n, at]
                )
                if dy == 0:
                    self.m["xb2", 0, n] = self.last_hop(
                        at_slot, self.B, self.last_xb.at[n], target, target_other
                    )
                else:
                    self.m["xb2", 1, n] = send(self.g.at[at_slot, self.B], self.xb2.at[n], target)

        def step_xa1(self):
            self.m["ya", 2].wait_recv()
            add_rows(self.na, self.rows_a(2), lambda at: self.ya.at[1, at])
            for n, target in enumerate((xp, xm)):
                self.m["xa1", n] = send(self.g.at[2, self.A, L[n]], self.xa1.at[n], target)

        def step_xa2(self):
            for n, (slot, target, target_other) in enumerate(((1, xp, xp_other), (3, xm, xm_other))):
                self.m["ya", slot].wait_recv()
                self.m["xa1", n].wait_recv()
                add_rows(
                    self.na, self.rows_a(slot, L[n]),
                    lambda at, n=n, slot=slot: self.ya.at[slot - 1, at, L[n]],
                    lambda at, n=n: self.xa1.at[n, at],
                )
                add_rows(
                    self.na, self.rows_a(slot, L[1 - n]),
                    lambda at, n=n, slot=slot: self.ya.at[slot - 1, at, L[1 - n]],
                )
                self.m["xa2", n] = self.last_hop(
                    slot, self.A, self.last_xa.at[n], target, target_other
                )

        def step_yb(self):
            for n in range(2):
                self.m["xb2", 1, n].wait_recv()
            add_rows(
                self.nb, self.rows_b(4),
                lambda at: self.xb2.at[0, at], lambda at: self.xb2.at[1, at],
            )
            self.m["yb"] = self.last_hop(4, self.B, self.last_yb, yp, yp_other)

        def total(self, rows, h, *received):
            mine = self.g[0, rows, lanes_of(core)].astype(F32)
            total = jnp.where(core == h, mine, self.own[rows, :].astype(F32))
            for part in received:
                total = total + part.astype(F32)
            return total * (1.0 / N_DP)

        def wait_last(self, *keys):
            for key in keys:
                for message in self.m[key]:
                    message.wait_recv()

        def write(self, out, value, fb, h):
            out[:, h, pl.ds(fb * HEAD, HEAD)] = value.T

        def finish_a(self, out):
            self.wait_last("own", ("ya", 0), ("xa2", 0), ("xa2", 1))
            for h in range(2):
                total = self.total(
                    self.A, h, self.last_ya[h], self.last_xa[0, h], self.last_xa[1, h]
                )
                self.sum_a[h] = total
                if self.na >= HEAD:
                    self.write(out, total[:HEAD], 0, h)

        def finish_b(self, out):
            self.wait_last(("xb2", 0, 0), ("xb2", 0, 1), "yb")
            done = self.na // HEAD
            for h in range(2):
                total = self.total(
                    self.B, h, self.last_yb[h], self.last_xb[0, h], self.last_xb[1, h]
                )
                rest = jnp.concatenate([self.sum_a[h, done * HEAD:, :], total], axis=0)
                for fb in range(done, self.width // HEAD):
                    at = (fb - done) * HEAD
                    self.write(out, rest[at:at + HEAD], fb, h)

    s_o = Scatter(
        go, HEAD, o_ya, o_xa1, o_xb1, o_xb2, o_own,
        o_last_ya, o_last_xa, o_last_yb, o_last_xb, o_sum_a,
    )
    s_q = Scatter(
        gq, QW, q_ya, q_xa1, q_xb1, q_xb2, q_own,
        q_last_ya, q_last_xa, q_last_yb, q_last_xb, q_sum_a,
    )

    def o_units(slot):
        weight_unit(go, ctx_t, up, slot)

    def backward(s):
        at = pl.ds(s * SEQ, SEQ)
        query, key, value = (qkv[at, pl.ds(n * HEAD, HEAD)] for n in range(3))
        grad_context = acc_o[at, :].astype(BF16)
        attn = probs[s]
        grad_prob = mm_nt(grad_context, value)
        row_dot = jnp.sum(attn * grad_prob, axis=-1, keepdims=True)
        grad_score = (attn * (grad_prob - row_dot) * scale).astype(BF16)
        query_t = query.astype(F32).T.astype(BF16)
        key_t = key.astype(F32).T.astype(BF16)
        grad_context_t = grad_context.astype(F32).T.astype(BF16)
        parts = (
            mm_nt(key_t, grad_score),
            mm(query_t, grad_score),
            mm(grad_context_t, attn.astype(BF16)),
        )
        for n, part in enumerate(parts):
            rows_t[pl.ds(n * HEAD, HEAD), at] = part.astype(BF16)
            lanes = pl.ds(n * HEAD, HEAD)
            if s == 0:
                rows[:, lanes] = part.T.astype(BF16)
            else:
                rows_other[:, lanes] = part.T.astype(BF16)

    def gn_group(g):
        share_msgs[SLOT_ORDER.index(g)].wait_recv()
        part = mm_nt(rows[...], wq[g].reshape(CHIP_D, 2 * QW)).astype(BF16)
        gn[g] = part.reshape(2, 128, CHIP_D)
        gn_step0(g)

    def z_rows(dz):
        return pl.ds(pl.multiple_of(lax.rem(z + dz + 8, 8) * 16, 16), 16)

    zm_msgs = {}
    directions = ((zp, 1), (zm, -1))

    def gn_step0(g):
        for n, (target, _) in enumerate(directions):
            zm_msgs[g, 0, n] = send(gn.at[g, n, z_rows(4)], zr0.at[n, g], target)

    def gn_step(g, step):
        for n, (target, sign) in enumerate(directions):
            at = z_rows(sign * (4 - step))
            zm_msgs[g, step - 1, n].wait_recv()
            if step == 1:
                mine = gn[g, n, at, :].astype(F32)
                gn[g, n, at, :] = (mine + zr0[n, g].astype(F32)).astype(BF16)
            else:
                mine = gn[g, :, at, :].astype(F32)
                gn[g, :, at, :] = (mine + zr1[n, g, step - 2].astype(F32)).astype(BF16)
            zm_msgs[g, step, n] = send(gn.at[g, :, at], zr1.at[n, g, step - 1], target)

    def gn_sum(g, which):
        total = gn[g, which, z_rows(0), :].astype(F32)
        return total + zr1[0, g, 2, which].astype(F32) + zr1[1, g, 2, which].astype(F32)

    def gn_exchange(g):
        for n in range(2):
            zm_msgs[g, 3, n].wait_recv()
        ysend[g] = gn_sum(g, 1 - yh).astype(BF16)
        zm_msgs[g, "y"] = send(ysend.at[g], yrecv.at[g], yhp)

    def gn_finish(g):
        zm_msgs[g, "y"].wait_recv()
        gnf[:, chip_cols(g)] = gn_sum(g, yh) + yrecv[g].astype(F32)

    def q_units(slot):
        weight_unit(gq, rows_t, nrm, slot)

    def norm_backward():
        total = gnf[...]
        standardized = xhat[...]
        mean_g = jnp.mean(total, axis=-1, keepdims=True)
        mean_p = jnp.mean(total * standardized, axis=-1, keepdims=True)
        hid_out[...] = (inv[:, :1] * (total - mean_g - standardized * mean_p)).astype(BF16)

    def await_up():
        loads[4].wait()
        up_msg.wait_recv()

    settled = []

    def settle(keep):
        for message in messages[len(settled):len(messages) - keep]:
            message.wait_send()
            settled.append(message)

    rows_msgs = []

    def share_rows():
        rows_msgs.append(send(rows_other, rows.at[:, pl.ds(QW, QW)], sib))

    def await_rows():
        rows_msgs[0].wait_recv()

    g_o.stage1()
    g_o.stage2()
    forward(0)
    await_up()
    forward(1)
    o_units(6)
    project_o(0)
    g_o.stage3()
    project_o(4)
    o_units(1)
    s_o.send_xb1(1)
    s_o.send_ya(2)
    o_units(4)
    o_units(5)
    o_units(7)
    o_units(3)
    g_o.stage4()
    o_units(2)
    g_o.stage5()
    project_o(3)
    s_o.send_ya(3)
    s_o.send_ya(1)
    project_o(1)
    s_o.send_ya(0)
    s_o.send_xb1(0)
    project_o(7)
    project_o(5)
    s_o.step_xa1()
    s_o.step_xb2(1)
    project_o(2)
    project_o(6)
    backward(1)
    share_rows()
    backward(0)
    q_units(6)
    s_q.send_ya(2)
    await_rows()
    s_q.send_xb1(1)
    gn_group(6)
    gn_group(5)
    gn_group(7)
    gn_group(2)
    q_units(2)
    s_q.send_xb1(0)
    q_units(7)
    gn_step(6, 1)
    gn_group(0)
    gn_step(5, 1)
    s_q.send_ya(3)
    gn_group(3)
    gn_step(7, 1)
    gn_step(2, 1)
    s_o.step_xb2(0)
    gn_group(4)
    gn_step(6, 2)
    s_q.step_xa1()
    q_units(5)
    s_q.send_ya(1)
    gn_step(5, 2)
    gn_group(1)
    gn_step(0, 1)
    s_q.step_xb2(1)
    gn_step(4, 1)
    gn_step(3, 1)
    gn_step(7, 2)
    q_units(4)
    q_units(3)
    s_q.send_ya(0)
    s_o.step_yb()
    gn_step(5, 3)
    gn_step(1, 1)
    gn_step(2, 2)
    gn_step(0, 2)
    q_units(1)
    gn_step(4, 2)
    s_o.step_xa2()
    gn_step(3, 2)
    s_q.step_xa2()
    gn_step(6, 3)
    gn_step(1, 2)
    gn_exchange(5)
    s_q.step_yb()
    gn_step(7, 3)
    gn_step(0, 3)
    gn_step(4, 3)
    s_q.step_xb2(0)
    o_units(0)
    gn_step(2, 3)
    gn_step(3, 3)
    q_units(0)
    s_o.send_own()
    gn_exchange(7)
    gn_step(1, 3)
    s_o.finish_a(go_out)
    gn_exchange(4)
    gn_exchange(6)
    gn_finish(5)
    s_q.send_own()
    gn_exchange(0)
    s_o.finish_b(go_out)
    gn_exchange(3)
    gn_exchange(2)
    gn_exchange(1)
    s_q.finish_a(gq_out)
    gn_finish(7)
    gn_finish(4)
    settle(24)
    gn_finish(6)
    s_q.finish_b(gq_out)
    gn_finish(3)
    gn_finish(0)
    gn_finish(2)
    gn_finish(1)
    norm_backward()

    settle(0)


def scatter_buffers(width):
    a = SCATTER_A[width]
    b = width - a
    return [
        pltpu.VMEM((3, a, CHIP_D), BF16),
        pltpu.VMEM((2, a, ROWS), BF16),
        pltpu.VMEM((2, 2, b, ROWS), BF16),
        pltpu.VMEM((2, b, CHIP_D), BF16),
        pltpu.VMEM((width, ROWS), BF16),
        pltpu.VMEM((2, a, ROWS), BF16),
        pltpu.VMEM((2, 2, a, ROWS), BF16),
        pltpu.VMEM((2, b, ROWS), BF16),
        pltpu.VMEM((2, 2, b, ROWS), BF16),
        pltpu.VMEM((2, a, ROWS), F32),
    ]


def hand_over_kernel(*refs):
    sources, targets, sem = refs[:3], refs[3:6], refs[6]
    copies = [
        pltpu.make_async_copy(a, b, sem.at[n]) for n, (a, b) in enumerate(zip(sources, targets))
    ]
    for copy in copies:
        copy.start()
    for copy in copies:
        copy.wait()


def hand_over(*arrays):
    return pl.pallas_call(
        hand_over_kernel,
        out_shape=tuple(jax.ShapeDtypeStruct(a.shape, a.dtype) for a in arrays),
        in_specs=[pl.BlockSpec(memory_space=pltpu.VMEM)] * 3,
        out_specs=(pl.BlockSpec(memory_space=pl.ANY),) * 3,
        scratch_shapes=[pltpu.SemaphoreType.DMA((3,))],
    )(*(pltpu.with_memory_space_constraint(a, pltpu.VMEM) for a in arrays))


def per_device(sublayer_input, w_qkv, w_out, upstream_grad):
    scratch = [
        pltpu.VMEM((ROWS, 2, QW), BF16),
        pltpu.VMEM((ROWS, 2, HEAD), BF16),
        pltpu.VMEM((2, ROWS, QW), BF16),
        pltpu.VMEM((2, ROWS, HEAD), BF16),
        pltpu.VMEM((N_CHIPS, 2, ROWS, 2 * QW), BF16),
        pltpu.VMEM((N_CHIPS, 2, ROWS, HEAD), BF16),
        pltpu.VMEM((2, SEQ, D), BF16),
        pltpu.VMEM((2, SEQ, D), BF16),
        pltpu.VMEM((SEQ, D), BF16),
        pltpu.VMEM((16, D), BF16),
        pltpu.VMEM((2 * SEQ, QW), F32),
        pltpu.VMEM((2 * SEQ, HEAD), F32),
        pltpu.VMEM((2 * SEQ, QW), BF16),
        pltpu.VMEM((2, SEQ, SEQ), F32),
        pltpu.VMEM((QW, 2 * SEQ), BF16),
        pltpu.VMEM((SEQ, 2 * QW), BF16),
        pltpu.VMEM((SEQ, QW), BF16),
        pltpu.VMEM((HEAD, 2 * SEQ), BF16),
        pltpu.VMEM((N_CHIPS, QW, CHIP_D), BF16),
        pltpu.VMEM((N_CHIPS, HEAD, CHIP_D), BF16),
        *scatter_buffers(QW),
        *scatter_buffers(HEAD),
        pltpu.VMEM((N_CHIPS, 2, 128, CHIP_D), BF16),
        pltpu.VMEM((2, GROUPS, 16, CHIP_D), BF16),
        pltpu.VMEM((2, GROUPS, 3, 2, 16, CHIP_D), BF16),
        pltpu.VMEM((GROUPS, 16, CHIP_D), BF16),
        pltpu.VMEM((GROUPS, 16, CHIP_D), BF16),
        pltpu.VMEM((16, D), F32),
        pltpu.VMEM((16, D), F32),
        pltpu.VMEM((16, 128), F32),
        pltpu.SemaphoreType.DMA((5,)),
        pltpu.SemaphoreType.DMA((N_MESSAGES,)),
        pltpu.SemaphoreType.DMA((N_MESSAGES,)),
    ]
    any_spec = pl.BlockSpec(memory_space=pl.ANY)
    vmem_spec = pl.BlockSpec(memory_space=pltpu.VMEM)
    hid, gq, go = pl.pallas_call(
        kernel,
        out_shape=(
            pltpu.VMEM((16, D), BF16),
            pltpu.VMEM((ROWS, 2, QW), F32),
            pltpu.VMEM((ROWS, 2, HEAD), F32),
        ),
        in_specs=[any_spec] * 4,
        out_specs=(vmem_spec,) * 3,
        scratch_shapes=scratch,
        compiler_params=pltpu.CompilerParams(
            collective_id=0, has_side_effects=True, vmem_limit_bytes=61 * 2**20
        ),
        cost_estimate=pl.CostEstimate(
            flops=10_000_000_000, bytes_accessed=10_000_000, transcendentals=200_000
        ),
    )(sublayer_input, w_qkv, w_out, upstream_grad)
    return hand_over(hid, gq, go)


def solution(mesh):
    in_specs = (P("dp", None), P("dp", "tensor", None), P("dp", "tensor", None), P("dp", None))
    out_specs = (P(("dp", "tensor"), None), P("dp", "tensor", None), P("dp", "tensor", None))
    return jax.shard_map(
        per_device, mesh=mesh, in_specs=in_specs, out_specs=out_specs, check_vma=False
    )
```

```python
import math

import jax
import jax.numpy as jnp
from jax import lax
from jax.experimental import pallas as pl
from jax.experimental.pallas import tpu as pltpu
from jax.sharding import PartitionSpec as P

EPS = 1e-05
MESH = pl.DeviceIdType.MESH
BF16 = jnp.bfloat16
F32 = jnp.float32

D = 6144
ROWS = 384
SEQ = 256
HEAD = 128
CHIP_D = 2 * ROWS
QW = 3 * HEAD
N_CHIPS = 8
N_DP = 16
GROUPS = 8
N_MESSAGES = 200
SLOT_ORDER = (0, 3, 1, 4, 7, 5, 2, 6)

GATHER_A, GATHER_A0, GATHER_B0 = 160, 80, 112
SCATTER_A = {QW: 160, HEAD: 48}


def mm(a, b):
    return lax.dot_general(a, b, (((1,), (0,)), ((), ())), preferred_element_type=F32)


def mm_nt(a, b):
    return lax.dot_general(a, b, (((1,), (1,)), ((), ())), preferred_element_type=F32)


def standardize(rows):
    centered = rows - jnp.mean(rows, axis=-1, keepdims=True)
    inverse_deviation = lax.rsqrt(jnp.mean(centered * centered, axis=-1, keepdims=True) + EPS)
    return centered * inverse_deviation, inverse_deviation


def kernel(
    x_hbm, wq_raw_hbm, wo_raw_hbm, up_hbm,
    hid_out, gq_out, go_out,
    wq_raw, wo_raw, wq_own, wo_own, wq, wo, nrm, up, xbuf, xrow, acc_q, acc_o, qkv, probs, rows_t, rows, rows_other, ctx_t,
    gq, go,
    q_ya, q_xa1, q_xb1, q_xb2, q_own, q_last_ya, q_last_xa, q_last_yb, q_last_xb, q_sum_a,
    o_ya, o_xa1, o_xb1, o_xb2, o_own, o_last_ya, o_last_xa, o_last_yb, o_last_xb, o_sum_a,
    gn, zr0, zr1, ysend, yrecv, gnf, xhat, inv,
    local_sem, send_sem, recv_sem,
):
    dp = lax.axis_index("dp")
    tn = lax.axis_index("tensor")
    core = lax.rem(dp, 2)
    other = 1 - core
    x = lax.rem(lax.div(dp, 2), 4)
    y = lax.div(dp, 8)
    z = lax.rem(tn, 8)
    yh = lax.div(tn, 8)

    def dp_at(yy, xx, cc):
        return (yy * 4 + xx) * 2 + cc

    sib = (dp_at(y, x, other), tn)
    xp = (dp_at(y, lax.rem(x + 1, 4), core), tn)
    xm = (dp_at(y, lax.rem(x + 3, 4), core), tn)
    yp = (dp_at(1 - y, x, core), tn)
    zp = (dp, yh * 8 + lax.rem(z + 1, 8))
    zm = (dp, yh * 8 + lax.rem(z + 7, 8))
    yhp = (dp, (1 - yh) * 8 + z)
    xp_other = (dp_at(y, lax.rem(x + 1, 4), other), tn)
    xm_other = (dp_at(y, lax.rem(x + 3, 4), other), tn)
    yp_other = (dp_at(1 - y, x, other), tn)
    partners = (sib, xp, xm, yp, zp, zm, yhp, xp_other, xm_other, yp_other)

    messages = []

    def send(src, dst, target):
        k = len(messages)
        copy = pltpu.make_async_remote_copy(
            src_ref=src, dst_ref=dst, send_sem=send_sem.at[k], recv_sem=recv_sem.at[k],
            device_id=target, device_id_type=MESH,
        )
        copy.start()
        messages.append(copy)
        return copy

    def chip_cols(slot):
        dy, dx = slot // 4, slot % 4
        chip = lax.rem(y + dy, 2) * 4 + lax.rem(x + dx, 4)
        return pl.ds(pl.multiple_of(chip * CHIP_D, 128), CHIP_D)

    def add_rows(n_rows, dst, *srcs):
        def body(r, carry):
            at = pl.ds(pl.multiple_of(r * 16, 16), 16)
            total = dst(at)[...].astype(F32)
            for src in srcs:
                total = total + src(at)[...].astype(F32)
            dst(at)[...] = total.astype(BF16)
            return carry

        lax.fori_loop(0, n_rows // 16, body, 0)

    barrier = pltpu.get_barrier_semaphore()
    for partner in partners:
        pl.semaphore_signal(barrier, inc=1, device_id=partner, device_id_type=MESH)
    token0 = pl.multiple_of(tn * 16, 16)
    loads = [
        pltpu.make_async_copy(x_hbm, xbuf, local_sem.at[0]),
        pltpu.make_async_copy(x_hbm.at[pl.ds(token0, 16)], xrow, local_sem.at[1]),
        pltpu.make_async_copy(
            wq_raw_hbm.at[pl.ds(0, GATHER_A)], wq_raw.at[pl.ds(0, GATHER_A)], local_sem.at[2]
        ),
        pltpu.make_async_copy(wo_raw_hbm, wo_raw, local_sem.at[3]),
        pltpu.make_async_copy(up_hbm, up.at[0], local_sem.at[4]),
        pltpu.make_async_copy(
            wq_raw_hbm.at[pl.ds(GATHER_A, ROWS - GATHER_A)],
            wq_raw.at[pl.ds(GATHER_A, ROWS - GATHER_A)],
            local_sem.at[5],
        ),
    ]
    loads[2].start()
    loads[5].start()
    loads[3].start()
    loads[2].wait()
    for h in range(2):
        wq_own[h, :GATHER_A] = wq_raw[:GATHER_A, h, :]
    own_loads = [
        pltpu.make_async_copy(wq_own.at[core], wq.at[0, core, :, pl.ds(0, QW)], local_sem.at[2]),
        pltpu.make_async_copy(wo_own.at[core], wo.at[0, core], local_sem.at[3]),
    ]
    pl.semaphore_wait(barrier, len(partners))

    A = pl.ds(0, GATHER_A)
    A0 = pl.ds(0, GATHER_A0)
    A1 = pl.ds(GATHER_A0, GATHER_A - GATHER_A0)
    B = pl.ds(GATHER_A, ROWS - GATHER_A)
    B0 = pl.ds(GATHER_A, GATHER_B0)
    B1 = pl.ds(GATHER_A + GATHER_B0, ROWS - GATHER_A - GATHER_B0)

    class Gather:
        def __init__(self, w, own, load, width, split):
            self.w, self.own, self.load, self.lanes = w, own, load, pl.ds(0, width)
            self.split = split

        def at(self, slot, rows, part=slice(None)):
            return self.w.at[slot, part, rows, self.lanes]

        def move(self, slot, rows, to_slot, target):
            return send(self.at(slot, rows), self.at(to_slot, rows), target)

        def stage0(self):
            src = self.own
            self.xa_p = [send(src.at[core, A], self.at(3, A, core), xp)]
            self.xa_m = [send(src.at[core, A], self.at(1, A, core), xm)]
            self.split()
            self.yb = [send(src.at[core, B], self.at(4, B, core), yp)]
            self.swap = send(src.at[other], self.at(0, slice(None), core), sib)
            self.load.start()

        def stage0b(self):
            self.swap.wait_recv()
            self.xa_p.append(send(self.at(0, A, other), self.at(3, A, other), xp))
            self.xa_m.append(send(self.at(0, A, other), self.at(1, A, other), xm))
            self.yb.append(send(self.at(0, B, other), self.at(4, B, other), yp))
            self.load.wait()
            self.xb_p = self.move(0, B, 3, xp)
            self.xb_m = self.move(0, B, 1, xm)
            self.ya0 = self.move(0, A, 4, yp)

        def stage1(self):
            for m in self.xa_p:
                m.wait_recv()
            self.xa2_p = self.move(3, A0, 2, xp)
            for m in self.xa_m:
                m.wait_recv()
            self.xa2_m = self.move(1, A1, 2, xm)
            self.ya3 = self.move(3, A, 7, yp)
            self.ya1 = self.move(1, A, 5, yp)

        def stage2(self):
            for m in self.yb:
                m.wait_recv()
            self.xb3_p = self.move(4, B, 7, xp)
            self.xb3_m = self.move(4, B, 5, xm)

        def stage3(self):
            self.xb_p.wait_recv()
            self.xb2_p = self.move(3, B0, 2, xp)
            self.xb_m.wait_recv()
            self.xb2_m = self.move(1, B1, 2, xm)

        def stage4(self):
            self.xa2_p.wait_recv()
            self.ya2_p = self.move(2, A0, 6, yp)
            self.xa2_m.wait_recv()
            self.ya2_m = self.move(2, A1, 6, yp)

        def stage5(self):
            self.xb3_p.wait_recv()
            self.xb4_p = self.move(7, B0, 6, xp)
            self.xb3_m.wait_recv()
            self.xb4_m = self.move(5, B1, 6, xm)

        def complete(self, slot):
            pending = {
                0: (), 3: (), 1: (), 4: (self.ya0,),
                2: (self.xb2_p, self.xb2_m) if slot == 2 else (),
                7: (self.ya3,), 5: (self.ya1,),
                6: (self.ya2_p, self.ya2_m, self.xb4_p, self.xb4_m) if slot == 6 else (),
            }[slot]
            for m in pending:
                m.wait_recv()

    def split_q():
        loads[5].wait()
        loads[0].start()
        loads[1].start()
        for h in range(2):
            wq_own[h, GATHER_A:] = wq_raw[GATHER_A:, h, :]

    def split_o():
        loads[3].wait()
        for h in range(2):
            wo_own[h] = wo_raw[:, h, :]

    g_q = Gather(wq, wq_own, own_loads[0], QW, split_q)
    g_o = Gather(wo, wo_own, own_loads[1], HEAD, lambda: None)
    g_q.stage0()
    split_o()
    g_q.stage0b()

    loads[0].wait()

    def norm_rows(r, carry):
        at = pl.ds(pl.multiple_of(r * 16, 16), 16)
        standardized, _ = standardize(xbuf[at, :].astype(F32))
        nrm[0, at, :] = standardized.astype(BF16)
        return carry

    lax.fori_loop(0, SEQ // 16, norm_rows, 0)
    nrm_msg = send(nrm.at[0], nrm.at[1], sib)

    def project(acc, w, left, width, slot):
        a = left[:, :, chip_cols(slot)].reshape(2 * SEQ, CHIP_D)
        product = mm(a, w[slot, :, :, pl.ds(0, width)].reshape(CHIP_D, width))
        if slot == 0:
            acc[...] = product
        else:
            acc[...] += product

    share_msgs = []

    def project_q(slot):
        g_q.complete(slot)
        share_msgs.append(send(
            wq.at[slot, :, :, pl.ds(0, QW)], wq.at[slot, :, :, pl.ds(QW, QW)], sib
        ))
        project(acc_q, wq, nrm, QW, slot)

    def project_o(slot):
        g_o.complete(slot)
        project(acc_o, wo, up, HEAD, slot)

    g_q.stage1()
    g_q.stage2()
    loads[4].start()
    up_msg = send(up_hbm, up.at[1], sib)
    loads[1].wait()
    own_xhat, own_inv = standardize(xrow[...].astype(F32))
    xhat[...] = own_xhat
    inv[...] = jnp.broadcast_to(own_inv, (16, 128))
    nrm_msg.wait_recv()
    project_q(0)
    g_q.stage3()
    project_q(3)
    g_q.stage4()
    project_q(1)
    project_q(4)
    g_q.stage5()
    g_o.stage0()
    project_q(7)
    g_o.stage0b()
    project_q(5)
    project_q(2)
    project_q(6)
    qkv[...] = acc_q[...].astype(BF16)

    scale = 1.0 / math.sqrt(HEAD)

    def forward(s):
        at = pl.ds(s * SEQ, SEQ)
        query, key, value = (qkv[at, pl.ds(n * HEAD, HEAD)] for n in range(3))
        raised = jnp.exp(mm_nt(query, key) * scale)
        attn = raised / jnp.sum(raised, axis=-1, keepdims=True)
        probs[s] = attn
        context = mm(attn.astype(BF16), value).astype(BF16).astype(F32)
        ctx_t[:, at] = context.T.astype(BF16)

    def weight_unit(g, left_t, right, slot):
        b = right[:, :, chip_cols(slot)].reshape(2 * SEQ, CHIP_D)
        g[slot] = mm(left_t[...], b).astype(BF16)

    L = (pl.ds(0, ROWS), pl.ds(ROWS, ROWS))

    def lanes_of(cc):
        return pl.ds(pl.multiple_of(cc * ROWS, 128), ROWS)

    class Scatter:
        def __init__(
            self, g, width, ya, xa1, xb1, xb2, own, last_ya, last_xa, last_yb, last_xb, sum_a
        ):
            self.g, self.width = g, width
            self.na = SCATTER_A[width]
            self.nb = width - self.na
            self.A, self.B = pl.ds(0, self.na), pl.ds(self.na, self.nb)
            self.ya, self.xa1, self.xb1, self.xb2, self.own = ya, xa1, xb1, xb2, own
            self.last_ya, self.last_xa, self.last_yb, self.last_xb = last_ya, last_xa, last_yb, last_xb
            self.sum_a = sum_a
            self.m = {}

        def rows_a(self, slot, lanes=slice(None)):
            return lambda at: self.g.at[slot, at, lanes]

        def rows_b(self, slot, lanes=slice(None)):
            def view(at):
                return self.g.at[slot, pl.ds(pl.multiple_of(at.start + self.na, 16), 16), lanes]

            return view

        def last_hop(self, slot, rows, buf, target, target_other):
            return [
                send(self.g.at[slot, rows, lanes_of(cc)], buf.at[core], to)
                for cc, to in ((core, target), (other, target_other))
            ]

        def send_own(self):
            self.m["own"] = [send(self.g.at[0, :, lanes_of(other)], self.own, sib)]

        def send_ya(self, dx):
            if dx == 0:
                self.m["ya", 0] = self.last_hop(4, self.A, self.last_ya, yp, yp_other)
            else:
                self.m["ya", dx] = send(self.g.at[4 + dx, self.A], self.ya.at[dx - 1], yp)

        def send_xb1(self, dy):
            for n, target in enumerate((xp, xm)):
                self.m["xb1", dy, n] = send(
                    self.g.at[dy * 4 + 2, self.B, L[n]], self.xb1.at[dy, n], target
                )

        def step_xb2(self, dy):
            for n, (slot, target, target_other) in enumerate(((1, xp, xp_other), (3, xm, xm_other))):
                self.m["xb1", dy, n].wait_recv()
                at_slot = dy * 4 + slot
                add_rows(
                    self.nb, self.rows_b(at_slot, L[n]), lambda at, n=n: self.xb1.at[dy, n, at]
                )
                if dy == 0:
                    self.m["xb2", 0, n] = self.last_hop(
                        at_slot, self.B, self.last_xb.at[n], target, target_other
                    )
                else:
                    self.m["xb2", 1, n] = send(self.g.at[at_slot, self.B], self.xb2.at[n], target)

        def step_xa1(self):
            self.m["ya", 2].wait_recv()
            add_rows(self.na, self.rows_a(2), lambda at: self.ya.at[1, at])
            for n, target in enumerate((xp, xm)):
                self.m["xa1", n] = send(self.g.at[2, self.A, L[n]], self.xa1.at[n], target)

        def step_xa2(self):
            for n, (slot, target, target_other) in enumerate(((1, xp, xp_other), (3, xm, xm_other))):
                self.m["ya", slot].wait_recv()
                self.m["xa1", n].wait_recv()
                add_rows(
                    self.na, self.rows_a(slot, L[n]),
                    lambda at, n=n, slot=slot: self.ya.at[slot - 1, at, L[n]],
                    lambda at, n=n: self.xa1.at[n, at],
                )
                add_rows(
                    self.na, self.rows_a(slot, L[1 - n]),
                    lambda at, n=n, slot=slot: self.ya.at[slot - 1, at, L[1 - n]],
                )
                self.m["xa2", n] = self.last_hop(
                    slot, self.A, self.last_xa.at[n], target, target_other
                )

        def step_yb(self):
            for n in range(2):
                self.m["xb2", 1, n].wait_recv()
            add_rows(
                self.nb, self.rows_b(4),
                lambda at: self.xb2.at[0, at], lambda at: self.xb2.at[1, at],
            )
            self.m["yb"] = self.last_hop(4, self.B, self.last_yb, yp, yp_other)

        def total(self, rows, h, *received):
            mine = self.g[0, rows, lanes_of(core)].astype(F32)
            total = jnp.where(core == h, mine, self.own[rows, :].astype(F32))
            for part in received:
                total = total + part.astype(F32)
            return total * (1.0 / N_DP)

        def wait_last(self, *keys):
            for key in keys:
                for message in self.m[key]:
                    message.wait_recv()

        def write(self, out, value, fb, h):
            out[:, h, pl.ds(fb * HEAD, HEAD)] = value.T

        def finish_a(self, out):
            self.wait_last("own", ("ya", 0), ("xa2", 0), ("xa2", 1))
            for h in range(2):
                total = self.total(
                    self.A, h, self.last_ya[h], self.last_xa[0, h], self.last_xa[1, h]
                )
                self.sum_a[h] = total
                if self.na >= HEAD:
                    self.write(out, total[:HEAD], 0, h)

        def finish_b(self, out):
            self.wait_last(("xb2", 0, 0), ("xb2", 0, 1), "yb")
            done = self.na // HEAD
            for h in range(2):
                total = self.total(
                    self.B, h, self.last_yb[h], self.last_xb[0, h], self.last_xb[1, h]
                )
                rest = jnp.concatenate([self.sum_a[h, done * HEAD:, :], total], axis=0)
                for fb in range(done, self.width // HEAD):
                    at = (fb - done) * HEAD
                    self.write(out, rest[at:at + HEAD], fb, h)

    s_o = Scatter(
        go, HEAD, o_ya, o_xa1, o_xb1, o_xb2, o_own,
        o_last_ya, o_last_xa, o_last_yb, o_last_xb, o_sum_a,
    )
    s_q = Scatter(
        gq, QW, q_ya, q_xa1, q_xb1, q_xb2, q_own,
        q_last_ya, q_last_xa, q_last_yb, q_last_xb, q_sum_a,
    )

    def o_units(slot):
        weight_unit(go, ctx_t, up, slot)

    def backward(s):
        at = pl.ds(s * SEQ, SEQ)
        query, key, value = (qkv[at, pl.ds(n * HEAD, HEAD)] for n in range(3))
        grad_context = acc_o[at, :].astype(BF16)
        attn = probs[s]
        grad_prob = mm_nt(grad_context, value)
        row_dot = jnp.sum(attn * grad_prob, axis=-1, keepdims=True)
        grad_score = (attn * (grad_prob - row_dot) * scale).astype(BF16)
        query_t = query.astype(F32).T.astype(BF16)
        key_t = key.astype(F32).T.astype(BF16)
        grad_context_t = grad_context.astype(F32).T.astype(BF16)
        parts = (
            mm_nt(key_t, grad_score),
            mm(query_t, grad_score),
            mm(grad_context_t, attn.astype(BF16)),
        )
        for n, part in enumerate(parts):
            rows_t[pl.ds(n * HEAD, HEAD), at] = part.astype(BF16)
            lanes = pl.ds(n * HEAD, HEAD)
            if s == 0:
                rows[:, lanes] = part.T.astype(BF16)
            else:
                rows_other[:, lanes] = part.T.astype(BF16)

    def gn_group(g):
        share_msgs[SLOT_ORDER.index(g)].wait_recv()
        part = mm_nt(rows[...], wq[g].reshape(CHIP_D, 2 * QW)).astype(BF16)
        gn[g] = part.reshape(2, 128, CHIP_D)
        gn_step0(g)

    def z_rows(dz):
        return pl.ds(pl.multiple_of(lax.rem(z + dz + 8, 8) * 16, 16), 16)

    zm_msgs = {}
    directions = ((zp, 1), (zm, -1))

    def gn_step0(g):
        for n, (target, _) in enumerate(directions):
            zm_msgs[g, 0, n] = send(gn.at[g, n, z_rows(4)], zr0.at[n, g], target)

    def gn_step(g, step):
        for n, (target, sign) in enumerate(directions):
            at = z_rows(sign * (4 - step))
            zm_msgs[g, step - 1, n].wait_recv()
            if step == 1:
                mine = gn[g, n, at, :].astype(F32)
                gn[g, n, at, :] = (mine + zr0[n, g].astype(F32)).astype(BF16)
            else:
                mine = gn[g, :, at, :].astype(F32)
                gn[g, :, at, :] = (mine + zr1[n, g, step - 2].astype(F32)).astype(BF16)
            zm_msgs[g, step, n] = send(gn.at[g, :, at], zr1.at[n, g, step - 1], target)

    def gn_sum(g, which):
        total = gn[g, which, z_rows(0), :].astype(F32)
        return total + zr1[0, g, 2, which].astype(F32) + zr1[1, g, 2, which].astype(F32)

    def gn_exchange(g):
        for n in range(2):
            zm_msgs[g, 3, n].wait_recv()
        ysend[g] = gn_sum(g, 1 - yh).astype(BF16)
        zm_msgs[g, "y"] = send(ysend.at[g], yrecv.at[g], yhp)

    def gn_finish(g):
        zm_msgs[g, "y"].wait_recv()
        gnf[:, chip_cols(g)] = gn_sum(g, yh) + yrecv[g].astype(F32)

    def q_units(slot):
        weight_unit(gq, rows_t, nrm, slot)

    def norm_backward():
        total = gnf[...]
        standardized = xhat[...]
        mean_g = jnp.mean(total, axis=-1, keepdims=True)
        mean_p = jnp.mean(total * standardized, axis=-1, keepdims=True)
        hid_out[...] = (inv[:, :1] * (total - mean_g - standardized * mean_p)).astype(BF16)

    def await_up():
        loads[4].wait()
        up_msg.wait_recv()

    settled = []

    def settle(keep):
        for message in messages[len(settled):len(messages) - keep]:
            message.wait_send()
            settled.append(message)

    rows_msgs = []

    def share_rows():
        rows_msgs.append(send(rows_other, rows.at[:, pl.ds(QW, QW)], sib))

    def await_rows():
        rows_msgs[0].wait_recv()

    g_o.stage1()
    g_o.stage2()
    forward(0)
    await_up()
    forward(1)
    o_units(6)
    project_o(0)
    g_o.stage3()
    project_o(4)
    o_units(1)
    s_o.send_xb1(1)
    s_o.send_ya(2)
    o_units(4)
    o_units(5)
    o_units(7)
    o_units(3)
    g_o.stage4()
    o_units(2)
    g_o.stage5()
    project_o(3)
    s_o.send_ya(3)
    s_o.send_ya(1)
    project_o(1)
    s_o.send_ya(0)
    s_o.send_xb1(0)
    project_o(7)
    project_o(5)
    s_o.step_xa1()
    s_o.step_xb2(1)
    project_o(2)
    project_o(6)
    backward(1)
    share_rows()
    backward(0)
    q_units(6)
    s_q.send_ya(2)
    await_rows()
    s_q.send_xb1(1)
    gn_group(6)
    gn_group(5)
    gn_group(7)
    gn_group(2)
    q_units(2)
    s_q.send_xb1(0)
    q_units(7)
    gn_step(6, 1)
    gn_group(0)
    gn_step(5, 1)
    s_q.send_ya(3)
    gn_group(3)
    gn_step(7, 1)
    gn_step(2, 1)
    s_o.step_xb2(0)
    gn_group(4)
    gn_step(6, 2)
    s_q.step_xa1()
    q_units(5)
    s_q.send_ya(1)
    gn_step(5, 2)
    gn_group(1)
    gn_step(0, 1)
    s_q.step_xb2(1)
    gn_step(4, 1)
    gn_step(3, 1)
    gn_step(7, 2)
    q_units(4)
    q_units(3)
    s_q.send_ya(0)
    s_o.step_yb()
    gn_step(5, 3)
    gn_step(1, 1)
    gn_step(2, 2)
    gn_step(0, 2)
    q_units(1)
    gn_step(4, 2)
    s_o.step_xa2()
    gn_step(3, 2)
    s_q.step_xa2()
    gn_step(6, 3)
    gn_step(1, 2)
    gn_exchange(5)
    s_q.step_yb()
    gn_step(7, 3)
    gn_step(0, 3)
    gn_step(4, 3)
    s_q.step_xb2(0)
    o_units(0)
    gn_step(2, 3)
    gn_step(3, 3)
    q_units(0)
    s_o.send_own()
    gn_exchange(7)
    gn_step(1, 3)
    s_o.finish_a(go_out)
    gn_exchange(4)
    gn_exchange(6)
    gn_finish(5)
    s_q.send_own()
    gn_exchange(0)
    s_o.finish_b(go_out)
    gn_exchange(3)
    gn_exchange(2)
    gn_exchange(1)
    s_q.finish_a(gq_out)
    gn_finish(7)
    gn_finish(4)
    settle(24)
    gn_finish(6)
    s_q.finish_b(gq_out)
    gn_finish(3)
    gn_finish(0)
    gn_finish(2)
    gn_finish(1)
    norm_backward()

    settle(0)


def scatter_buffers(width):
    a = SCATTER_A[width]
    b = width - a
    return [
        pltpu.VMEM((3, a, CHIP_D), BF16),
        pltpu.VMEM((2, a, ROWS), BF16),
        pltpu.VMEM((2, 2, b, ROWS), BF16),
        pltpu.VMEM((2, b, CHIP_D), BF16),
        pltpu.VMEM((width, ROWS), BF16),
        pltpu.VMEM((2, a, ROWS), BF16),
        pltpu.VMEM((2, 2, a, ROWS), BF16),
        pltpu.VMEM((2, b, ROWS), BF16),
        pltpu.VMEM((2, 2, b, ROWS), BF16),
        pltpu.VMEM((2, a, ROWS), F32),
    ]


def hand_over_kernel(*refs):
    sources, targets, sem = refs[:3], refs[3:6], refs[6]
    copies = [
        pltpu.make_async_copy(a, b, sem.at[n]) for n, (a, b) in enumerate(zip(sources, targets))
    ]
    for copy in copies:
        copy.start()
    for copy in copies:
        copy.wait()


def hand_over(*arrays):
    return pl.pallas_call(
        hand_over_kernel,
        out_shape=tuple(jax.ShapeDtypeStruct(a.shape, a.dtype) for a in arrays),
        in_specs=[pl.BlockSpec(memory_space=pltpu.VMEM)] * 3,
        out_specs=(pl.BlockSpec(memory_space=pl.ANY),) * 3,
        scratch_shapes=[pltpu.SemaphoreType.DMA((3,))],
    )(*(pltpu.with_memory_space_constraint(a, pltpu.VMEM) for a in arrays))


def per_device(sublayer_input, w_qkv, w_out, upstream_grad):
    scratch = [
        pltpu.VMEM((ROWS, 2, QW), BF16),
        pltpu.VMEM((ROWS, 2, HEAD), BF16),
        pltpu.VMEM((2, ROWS, QW), BF16),
        pltpu.VMEM((2, ROWS, HEAD), BF16),
        pltpu.VMEM((N_CHIPS, 2, ROWS, 2 * QW), BF16),
        pltpu.VMEM((N_CHIPS, 2, ROWS, HEAD), BF16),
        pltpu.VMEM((2, SEQ, D), BF16),
        pltpu.VMEM((2, SEQ, D), BF16),
        pltpu.VMEM((SEQ, D), BF16),
        pltpu.VMEM((16, D), BF16),
        pltpu.VMEM((2 * SEQ, QW), F32),
        pltpu.VMEM((2 * SEQ, HEAD), F32),
        pltpu.VMEM((2 * SEQ, QW), BF16),
        pltpu.VMEM((2, SEQ, SEQ), F32),
        pltpu.VMEM((QW, 2 * SEQ), BF16),
        pltpu.VMEM((SEQ, 2 * QW), BF16),
        pltpu.VMEM((SEQ, QW), BF16),
        pltpu.VMEM((HEAD, 2 * SEQ), BF16),
        pltpu.VMEM((N_CHIPS, QW, CHIP_D), BF16),
        pltpu.VMEM((N_CHIPS, HEAD, CHIP_D), BF16),
        *scatter_buffers(QW),
        *scatter_buffers(HEAD),
        pltpu.VMEM((N_CHIPS, 2, 128, CHIP_D), BF16),
        pltpu.VMEM((2, GROUPS, 16, CHIP_D), BF16),
        pltpu.VMEM((2, GROUPS, 3, 2, 16, CHIP_D), BF16),
        pltpu.VMEM((GROUPS, 16, CHIP_D), BF16),
        pltpu.VMEM((GROUPS, 16, CHIP_D), BF16),
        pltpu.VMEM((16, D), F32),
        pltpu.VMEM((16, D), F32),
        pltpu.VMEM((16, 128), F32),
        pltpu.SemaphoreType.DMA((6,)),
        pltpu.SemaphoreType.DMA((N_MESSAGES,)),
        pltpu.SemaphoreType.DMA((N_MESSAGES,)),
    ]
    any_spec = pl.BlockSpec(memory_space=pl.ANY)
    vmem_spec = pl.BlockSpec(memory_space=pltpu.VMEM)
    hid, gq, go = pl.pallas_call(
        kernel,
        out_shape=(
            pltpu.VMEM((16, D), BF16),
            pltpu.VMEM((ROWS, 2, QW), F32),
            pltpu.VMEM((ROWS, 2, HEAD), F32),
        ),
        in_specs=[any_spec] * 4,
        out_specs=(vmem_spec,) * 3,
        scratch_shapes=scratch,
        compiler_params=pltpu.CompilerParams(
            collective_id=0, has_side_effects=True, vmem_limit_bytes=61 * 2**20
        ),
        cost_estimate=pl.CostEstimate(
            flops=10_000_000_000, bytes_accessed=10_000_000, transcendentals=200_000
        ),
    )(sublayer_input, w_qkv, w_out, upstream_grad)
    return hand_over(hid, gq, go)


def solution(mesh):
    in_specs = (P("dp", None), P("dp", "tensor", None), P("dp", "tensor", None), P("dp", None))
    out_specs = (P(("dp", "tensor"), None), P("dp", "tensor", None), P("dp", "tensor", None))
    return jax.shard_map(
        per_device, mesh=mesh, in_specs=in_specs, out_specs=out_specs, check_vma=False
    )
```
